128 devices in a mesh: row: 8 (over z, core), col: 16 (over y, x).
Axes of the slice: x: 4, y: 4, z: 4, core: 2. Of those that a mesh axis runs over, the one named last changes fastest.
Arguments:
- signal_frames: bfloat16 [65536, 768], P(('row', 'col')), may hold values from -6 to 6
- triple_projection_factors: bfloat16 [768, 2304], replicated, may hold values from -0.21875 to 0.21875
- mixing_projection_factors: bfloat16 [768, 768], replicated, may hold values from -0.21875 to 0.21875
- logit_scaling: float32 [12], replicated, may hold values from 2 to 16
- dispatcher_columns: bfloat16 [768, 256], replicated, may hold values from -0.21875 to 0.21875
- specialist_pick: int32 [65536, 1], P(('row', 'col')), may hold values from 0 to 255; in each aligned block of 512 rows (0 to 511, 512 to 1023, ...) at most 3 rows name the same one
- specialist_entry_factors: bfloat16 [256, 768, 3072], P(('row', 'col')), may hold values from -0.21875 to 0.21875
- specialist_exit_factors: bfloat16 [256, 3072, 768], P(('row', 'col')), may hold values from -0.109375 to 0.109375
Outputs:
- encoded: bfloat16 [65536, 768], P(('row', 'col'))
The draws below stay inside these ranges and needn't reach their ends.
Inputs may be any that keep to these rules, and one draw needn't show every extreme that they name: `specialist_pick`: within each aligned block of 512 rows no expert is chosen more than 3 times, a bound that some block reaches; every expert is chosen by some row.
All inputs are finite; a program needn't handle non-finite values.
Results may differ from the reference program's by a relative error of at most 0.0056.
Values may be sent and summed in bfloat16 or wider, within the bound.
No kernel may reach another device: no remote copies, remote signals or barrier semaphores. Data moves between devices by JAX's collectives and lax.ppermute only.
A program may use at most 128 MiB of HBM per device.

```python
import math
import jax
import jax.numpy as jnp
import numpy as np
from jax import lax

D = 768
PROBE_TOTAL = 12
FF = 3072
TOK_DEV = 512
LOOKBACK_SPAN = 256
EXPERTS = 256
CAP = 3
TOKENS = 65536
N_ROW = 8
N_COL = 16


def levels(stream_key, dims, pieces, smallest, largest):
    def one(position, shards_of):
        steps = jax.random.uniform(jax.random.fold_in(jax.random.fold_in(stream_key, 6), position), (shards_of,), jnp.float32, smallest / len(pieces), largest / len(pieces))
        return jnp.repeat(jnp.exp(steps), dims[position] // shards_of).reshape((-1,) + (1,) * (len(dims) - position - 1))

    loudness = one(*pieces[0])
    for cut in pieces[1:]:
        loudness = loudness * one(*cut)
    return loudness


def assign_block(own_key, own, number, rows, number_of, top, reach, slope):
    sequence = jax.random.permutation(own_key, number_of)
    packed, common = shares(number_of, rows * top, reach, slope, True), shares(number_of, rows * top, reach, slope, False)
    places = jnp.arange(number_of)

    def named(tallies, offset_by):
        used = int((tallies > 0).sum())
        fixed = max(1, used // 4)
        moved = fixed + (places - fixed + offset_by * (used - fixed)) % max(1, number_of - fixed)
        return jnp.zeros((number_of,), jnp.int32).at[sequence[jnp.where(places < fixed, places, moved)]].set(jnp.asarray(tallies, jnp.int32))

    tallies = jnp.where(number % 4 == 0, named(packed, number // 4), named(common, number - number // 4 - 1))
    mixed = jax.random.permutation(jax.random.fold_in(own, 3), number_of)
    donor, sink = mixed[0:number_of // 2 * 2:2], mixed[1:number_of // 2 * 2:2]
    room = jnp.minimum(tallies[donor] - 1, reach - tallies[sink]) // 2
    room = jnp.where((donor == sequence[0]) | (sink == sequence[0]) | (tallies[sink] == 0), 0, jnp.maximum(room, 0))
    moved = jax.random.randint(jax.random.fold_in(own, 4), (number_of // 2,), 0, 1 << 20) % (room + 1)
    tallies = tallies.at[donor].add(-moved).at[sink].add(moved)
    labels = jnp.searchsorted(jnp.cumsum(tallies), jnp.arange(rows * top), side="right").astype(jnp.int32)
    grid = labels.reshape(top, rows).T
    grid = grid[jax.random.permutation(jax.random.fold_in(own, 1), rows)]
    offset_by = jax.random.randint(jax.random.fold_in(own, 2), (rows, 1), 0, top)
    return jnp.take_along_axis(grid, (jnp.arange(top)[None, :] + offset_by) % top, axis=1)


def shares(count, total, reach, lean, full):
    weights = [(1 << 20) // math.isqrt(grade ** lean) + 1 for grade in range(1, count + 1)]
    largest = reach if full else min(reach, max(-(-total // count), total * weights[0] // sum(weights)))
    least = 1 if total - largest >= count - 1 else 0
    given, spare = [largest] + [least] * (count - 1), total - largest - least * (count - 1)
    while spare > 0:
        free = [i for i in range(1, count) if given[i] < largest] or [i for i in range(1, count) if given[i] < reach]
        pool, budget = sum([weights[i] for i in free]), spare
        for i in free:
            addition = min(reach - given[i], max(1, budget * weights[i] // pool), spare)
            given[i] = given[i] + addition
            spare = spare - addition
    return np.array(given)


def bell_draw(own_key, extent, width, reach, cuts=(), kind=jnp.bfloat16):
    factor_of = levels(own_key, extent, cuts, -0.22, 0.18) if cuts else 1.0
    entries = jax.random.normal(own_key, extent, jnp.float32) * width * factor_of
    return jnp.minimum(jnp.maximum(entries, -reach), reach).astype(kind)


def setup_inputs(seed: int = 0) -> dict:
    key_of = jax.random.split(jax.random.key(seed), 9)
    signal_frames = bell_draw(key_of[0], (TOKENS, D), 1.0, 6.0, ((0, 128),))
    triple_projection_factors = bell_draw(key_of[1], (D, 3 * D), D ** -0.5, 0.21875)
    mixing_projection_factors = bell_draw(key_of[2], (D, D), D ** -0.5, 0.21875)
    logit_scaling = jnp.clip(jnp.exp(jax.random.uniform(key_of[3], (PROBE_TOTAL,), jnp.float32, math.log(2.0), math.log(16.0))), 2.0, 16.0)
    dispatcher_columns = bell_draw(key_of[4], (D, EXPERTS), D ** -0.5, 0.21875)
    specialist_pick_keys = jax.random.split(jax.random.fold_in(key_of[5], 1), TOKENS // TOK_DEV)
    specialist_pick_turns = jax.random.permutation(jax.random.fold_in(key_of[5], 3), TOKENS // TOK_DEV)
    specialist_pick = jax.vmap(lambda own, number: assign_block(jax.random.fold_in(key_of[5], 2), own, number, TOK_DEV, EXPERTS, 1, CAP, 2))(specialist_pick_keys, specialist_pick_turns).reshape((TOKENS, 1))
    specialist_entry_factors = bell_draw(key_of[6], (EXPERTS, D, FF), D ** -0.5, 0.21875, ((0, 128),))
    specialist_exit_factors = bell_draw(key_of[7], (EXPERTS, FF, D), FF ** -0.5, 0.109375, ((0, 128),))
    return {"signal_frames": signal_frames, "triple_projection_factors": triple_projection_factors, "mixing_projection_factors": mixing_projection_factors, "logit_scaling": logit_scaling, "dispatcher_columns": dispatcher_columns, "specialist_pick": specialist_pick, "specialist_entry_factors": specialist_entry_factors, "specialist_exit_factors": specialist_exit_factors}


def layer_norm(matrix):
    matrix = matrix.astype(jnp.float32)
    center = matrix - lax.optimization_barrier(jnp.mean(matrix, axis=-1, keepdims=True))
    spread = lax.optimization_barrier(jnp.mean(center * center, axis=-1, keepdims=True))
    return (center * lax.rsqrt(spread + 1e-05)).astype(jnp.bfloat16)

def head_norm(matrix):
    count = matrix.shape[0]
    split = matrix.reshape(count, PROBE_TOTAL, D // PROBE_TOTAL)
    scaled = split * lax.rsqrt(lax.optimization_barrier(jnp.mean(split * split, axis=-1, keepdims=True)) + 1e-06)
    return scaled.reshape(count, D).astype(jnp.bfloat16)

def local_similarity_pass(asker_tile_entries, lookup_tile_entries, payload_tile_entries, logit_scaling, asker_start_position, lookup_start_position):
    n_query = asker_tile_entries.shape[0]
    n_key = lookup_tile_entries.shape[0]
    probe_dimension = D // PROBE_TOTAL
    raw_similarity_logits = jnp.einsum('qhd,khd->hqk', asker_tile_entries.reshape(n_query, PROBE_TOTAL, probe_dimension).astype(jnp.float32), lookup_tile_entries.reshape(n_key, PROBE_TOTAL, probe_dimension).astype(jnp.float32))
    similarity_logits = logit_scaling[:, None, None] * raw_similarity_logits / probe_dimension
    query_pos = asker_start_position + jnp.arange(n_query, dtype=jnp.int32)
    key_pos = lookup_start_position + jnp.arange(n_key, dtype=jnp.int32)
    permitted_pairs = (key_pos[None, :] <= query_pos[:, None]) & (key_pos[None, :] >= query_pos[:, None] - LOOKBACK_SPAN) & (key_pos[None, :] >= 0)
    specialist_results = jnp.where(permitted_pairs[None], jnp.exp(similarity_logits - logit_scaling[:, None, None]), 0.0)
    weights = (specialist_results / lax.optimization_barrier(jnp.sum(specialist_results, axis=-1, keepdims=True))).astype(jnp.bfloat16)
    context = jnp.einsum('hqk,khd->qhd', weights.astype(jnp.float32), payload_tile_entries.reshape(n_key, PROBE_TOTAL, probe_dimension).astype(jnp.float32))
    return context.reshape(n_query, D).astype(jnp.bfloat16)

def reference(signal_frames, triple_projection_factors, mixing_projection_factors, logit_scaling, dispatcher_columns, specialist_pick, specialist_entry_factors, specialist_exit_factors):
    devices = N_ROW * N_COL
    normed = layer_norm(signal_frames)
    projected = jnp.dot(normed, triple_projection_factors, preferred_element_type=jnp.float32)
    asker_tile_entries = head_norm(projected[:, :D])
    lookup_tile_entries = head_norm(projected[:, D:2 * D])
    payload_tile_entries = projected[:, 2 * D:].astype(jnp.bfloat16)
    key_padded = jnp.concatenate([jnp.zeros((LOOKBACK_SPAN, D), lookup_tile_entries.dtype), lookup_tile_entries], axis=0)
    value_padded = jnp.concatenate([jnp.zeros((LOOKBACK_SPAN, D), payload_tile_entries.dtype), payload_tile_entries], axis=0)

    def one_block(block_index):
        lookback_shift = (block_index * TOK_DEV).astype(jnp.int32)
        asker_segment = lax.dynamic_slice_in_dim(asker_tile_entries, lookback_shift, TOK_DEV, 0)
        lookup_segment = lax.dynamic_slice_in_dim(key_padded, lookback_shift, TOK_DEV + LOOKBACK_SPAN, 0)
        payload_segment = lax.dynamic_slice_in_dim(value_padded, lookback_shift, TOK_DEV + LOOKBACK_SPAN, 0)
        return local_similarity_pass(asker_segment, lookup_segment, payload_segment, logit_scaling, lookback_shift, lookback_shift - LOOKBACK_SPAN)
    context = lax.map(one_block, jnp.arange(devices, dtype=jnp.int32)).reshape(TOKENS, D)
    hidden = (signal_frames.astype(jnp.float32) + jnp.dot(context, mixing_projection_factors, preferred_element_type=jnp.float32)).astype(jnp.bfloat16)
    routed = layer_norm(hidden)
    logits = jnp.dot(routed, dispatcher_columns, preferred_element_type=jnp.float32)
    chosen = specialist_pick[:, 0]
    onehot = chosen[:, None] == jnp.arange(EXPERTS, dtype=jnp.int32)[None, :]
    gate_value = jax.nn.sigmoid(lax.optimization_barrier(jnp.sum(jnp.where(onehot, logits, 0.0), axis=1)))
    counts = jnp.cumsum(onehot.astype(jnp.int32).reshape(devices, TOK_DEV, EXPERTS), axis=1).reshape(TOKENS, EXPERTS)
    slot_index = lax.optimization_barrier(jnp.sum(jnp.where(onehot, counts - 1, 0), axis=1)).astype(jnp.int32)
    block_of = jnp.arange(TOKENS, dtype=jnp.int32) // TOK_DEV
    flat_index = ((block_of * EXPERTS + chosen) * CAP + slot_index).astype(jnp.int32)
    buffer = jnp.zeros((devices * EXPERTS * CAP, D), routed.dtype).at[flat_index].set(routed)
    grouped = buffer.reshape(devices, EXPERTS, CAP, D).transpose(1, 0, 2, 3).reshape(EXPERTS, devices * CAP, D)

    def one_expert(operands):
        expert_rows, first_weight, second_weight = operands
        expert_hidden = jax.nn.relu(jnp.dot(expert_rows, first_weight, preferred_element_type=jnp.float32)).astype(jnp.bfloat16)
        return jnp.dot(expert_hidden, second_weight, preferred_element_type=jnp.float32).astype(jnp.bfloat16)
    expert_out = lax.map(one_expert, (grouped, specialist_entry_factors, specialist_exit_factors))
    returned = expert_out.reshape(EXPERTS, devices, CAP, D).transpose(1, 0, 2, 3).reshape(devices * EXPERTS * CAP, D)
    picked = returned[flat_index]
    return (hidden.astype(jnp.float32) + gate_value[:, None] * picked.astype(jnp.float32)).astype(jnp.bfloat16)
```

```python
import math

import jax
import jax.numpy as jnp
from jax import lax
from jax.experimental import pallas as pl
from jax.experimental.pallas import tpu as pltpu
from jax.sharding import PartitionSpec as P

D = 768
HEADS = 12
LOOK = 256
T = 512
FF = 3072
CAP = 3
SLOTS = 768
PAIRS = HEADS // 2
LANES = 128
AXES = ("row", "col")
BF = jnp.bfloat16
F32 = jnp.float32
MB = 1 << 20


def dot(a, b):
    return jnp.dot(a, b, preferred_element_type=F32)


def dot_t(a, b):
    return lax.dot_general(a, b, (((1,), (1,)), ((), ())), preferred_element_type=F32)


def norm_rows(value):
    center = value - jnp.mean(value, axis=-1, keepdims=True)
    spread = jnp.mean(center * center, axis=-1, keepdims=True)
    return (center * lax.rsqrt(spread + 1e-05)).astype(BF)


def head_blocks():
    down = lax.shift_right_logical(lax.broadcasted_iota(jnp.int32, (256, 256), 0), 6)
    across = lax.shift_right_logical(lax.broadcasted_iota(jnp.int32, (256, 256), 1), 6)
    return jnp.where(down == across, 1.0, 0.0).astype(BF)


def head_norm(value, blocks):
    square = (value * value).astype(BF)
    return value * lax.rsqrt(dot(square, blocks) * (1.0 / 64) + 1e-06)


def triangles():
    down = lax.broadcasted_iota(jnp.int32, (128, 128), 0)
    across = lax.broadcasted_iota(jnp.int32, (128, 128), 1)
    behind = jnp.where(across >= down, 1.0, 0.0).astype(BF)
    ahead = jnp.where(across <= down, 1.0, 0.0).astype(BF)
    return behind, ahead


def half_lanes(half):
    lane = lax.broadcasted_iota(jnp.int32, (1, LANES), 1)
    mine = (lane < 64) if half == 0 else (lane >= 64)
    return jnp.where(mine, 1.0, 0.0).astype(BF)


def weigh(part):
    return jnp.exp2(part).astype(BF)


def behind_weights(scores, behind):
    top = jnp.concatenate([weigh(scores[:128, :128]) * behind, weigh(scores[:128, 128:])], axis=1)
    low = jnp.concatenate([jnp.zeros((128, 128), BF), weigh(scores[128:, 128:]) * behind], axis=1)
    return jnp.concatenate([top, low], axis=0)


def own_weights(scores, ahead):
    top = jnp.concatenate([weigh(scores[:128, :128]) * ahead, jnp.zeros((128, 128), BF)], axis=1)
    low = jnp.concatenate([weigh(scores[128:, :128]), weigh(scores[128:, 128:]) * ahead], axis=1)
    return jnp.concatenate([top, low], axis=0)


def payload(values, half, ones):
    mask = half_lanes(half)
    return jnp.concatenate([values * mask, ones * mask], axis=1)


def first_kernel(x_ref, w_ref, mix_ref, scale_ref, q_out, acc_out, hid_out, rou_out, normed, q_s, k_s, v_s, ctx):
    for r in range(0, T, 32):
        normed[r : r + 32, :] = norm_rows(x_ref[r : r + 32, :].astype(F32))
    blocks = head_blocks()
    for g in range(3):
        c = slice(g * 256, g * 256 + 256)
        value = head_norm(dot(normed[...], w_ref[:, g * 256 : g * 256 + 256]), blocks)
        q_s[:, c] = (value * scale_ref[:, c]).astype(BF)
        value = head_norm(dot(normed[...], w_ref[:, D + g * 256 : D + g * 256 + 256]), blocks)
        k_s[:, c] = value.astype(BF)
        v_s[:, c] = dot(normed[...], w_ref[:, 2 * D + g * 256 : 2 * D + g * 256 + 256]).astype(BF)
    q_out[...] = q_s[:LOOK, :]
    behind, ahead = triangles()
    ones = jnp.ones((LOOK, LANES), BF)
    for pair in range(PAIRS):
        c = slice(pair * LANES, pair * LANES + LANES)
        low = jnp.zeros((LOOK, 256), F32)
        high = jnp.zeros((LOOK, 256), F32)
        for half in range(2):
            mask = half_lanes(half)
            q0 = q_s[:LOOK, c] * mask
            q1 = q_s[LOOK:, c] * mask
            k0 = k_s[:LOOK, c]
            k1 = k_s[LOOK:, c]
            v0 = payload(v_s[:LOOK, c], half, ones)
            v1 = payload(v_s[LOOK:, c], half, ones)
            low += dot(own_weights(dot_t(q0, k0), ahead), v0)
            high += dot(behind_weights(dot_t(q1, k0), behind), v0)
            high += dot(own_weights(dot_t(q1, k1), ahead), v1)
        acc_out[:, pair * 256 : pair * 256 + 256] = low
        ctx[:, c] = (high[:, :LANES] / high[:, LANES:]).astype(BF)
    finish(ctx, mix_ref, x_ref, LOOK, hid_out, rou_out, 0)


def finish(ctx, mix_ref, x_ref, x_at, hid_out, rou_out, at):
    for r in range(0, LOOK, 128):
        mixed = dot(ctx[r : r + 128, :], mix_ref[...])
        for s in range(r, r + 128, 32):
            hidden = (x_ref[x_at + s : x_at + s + 32, :].astype(F32) + mixed[s - r : s - r + 32, :]).astype(BF)
            hid_out[at + s : at + s + 32, :] = hidden
            rou_out[at + s : at + s + 32, :] = norm_rows(hidden.astype(F32))


def second_kernel(valid_ref, halo_ref, w_ref, mix_ref, x_ref, q_ref, acc_ref, hid_ref, rou_ref, row_ref, buf_out, hid_out, rou_out, normed, k_s, v_s, ctx):
    for r in range(0, LOOK, 32):
        normed[r : r + 32, :] = norm_rows(halo_ref[r : r + 32, :].astype(F32))
    blocks = head_blocks()
    for g in range(3):
        c = slice(g * 256, g * 256 + 256)
        k_s[:, c] = head_norm(dot(normed[...], w_ref[:, D + g * 256 : D + g * 256 + 256]), blocks).astype(BF)
        v_s[:, c] = dot(normed[...], w_ref[:, 2 * D + g * 256 : 2 * D + g * 256 + 256]).astype(BF)
    behind, _ = triangles()
    ones = jnp.full((LOOK, LANES), valid_ref[0].astype(F32)).astype(BF)
    for pair in range(PAIRS):
        c = slice(pair * LANES, pair * LANES + LANES)
        low = acc_ref[:, pair * 256 : pair * 256 + 256]
        for half in range(2):
            q0 = q_ref[:, c] * half_lanes(half)
            low += dot(behind_weights(dot_t(q0, k_s[:, c]), behind), payload(v_s[:, c] * ones, half, ones))
        ctx[:, c] = (low[:, :LANES] / low[:, LANES:]).astype(BF)
    finish(ctx, mix_ref, x_ref, 0, hid_out, rou_out, 0)
    hid_out[LOOK:, :] = hid_ref[...]
    rou_out[LOOK:, :] = rou_ref[...]
    for s in range(0, SLOTS, 256):
        place = lax.broadcasted_iota(jnp.int32, (256, T), 0) + s
        pick = jnp.where(place == row_ref[...], 1.0, 0.0).astype(BF)
        buf_out[s : s + 256, :] = dot(pick, rou_out[...]).astype(BF)


def expert_kernel(in_ref, first_ref, second_ref, out_ref, rows, total, done):
    expert = pl.program_id(0)
    chunk = pl.program_id(1)

    @pl.when(chunk == 0)
    def _():
        down = lax.broadcasted_iota(jnp.int32, (128, 256), 0)
        across = lax.broadcasted_iota(jnp.int32, (128, 256), 1)
        pick = jnp.where(across == 2 * down + expert, 1.0, 0.0).astype(BF)
        for b in range(3):
            rows[b * 128 : b * 128 + 128, :] = dot(pick, in_ref[b * 256 : b * 256 + 256, :]).astype(BF)

    hidden = jnp.maximum(dot(rows[...], first_ref[0]), 0.0).astype(BF)
    part = dot(hidden, second_ref[0])

    @pl.when(chunk == 0)
    def _():
        total[...] = part

    @pl.when(chunk > 0)
    def _():
        total[...] += part

    @pl.when(chunk == pl.num_programs(1) - 1)
    def _():
        done[expert] = total[...].astype(BF)

    @pl.when((chunk == pl.num_programs(1) - 1) & (expert == 1))
    def _():
        down = lax.broadcasted_iota(jnp.int32, (256, 128), 0)
        across = lax.broadcasted_iota(jnp.int32, (256, 128), 1)
        put0 = jnp.where(down == 2 * across, 1.0, 0.0).astype(BF)
        put1 = jnp.where(down == 2 * across + 1, 1.0, 0.0).astype(BF)
        for b in range(3):
            r = slice(b * 128, b * 128 + 128)
            out_ref[b * 256 : b * 256 + 256, :] = (dot(put0, done[0, r, :]) + dot(put1, done[1, r, :])).astype(BF)


def gate_kernel(rou_ref, columns_ref, pick_ref, gate_out):
    logits = dot(rou_ref[...], columns_ref[...])
    across = lax.broadcasted_iota(jnp.int32, logits.shape, 1)
    chosen = jnp.sum(jnp.where(across == pick_ref[...], logits, 0.0), axis=1, keepdims=True)
    gate_out[...] = 1.0 / (1.0 + jnp.exp(-chosen))


def last_kernel(back_ref, hid_ref, gate_ref, col_ref, out_ref):
    for r in range(0, T, 256):
        across = lax.broadcasted_iota(jnp.int32, (256, SLOTS), 1)
        pick = jnp.where(across == col_ref[r : r + 256, :], 1.0, 0.0).astype(BF)
        picked = dot(pick, back_ref[...])
        gate = gate_ref[r : r + 256, :]
        out_ref[r : r + 256, :] = (hid_ref[r : r + 256, :].astype(F32) + gate * picked).astype(BF)


def params(limit):
    return pltpu.CompilerParams(vmem_limit_bytes=limit * MB)


def shape(*dims, dtype=BF):
    return jax.ShapeDtypeStruct(dims, dtype)


def cost(flops, moved, exps=0):
    return pl.CostEstimate(flops=flops, bytes_accessed=moved, transcendentals=exps)


def shards(x, triple, mixing, scaling, columns, pick, entry, exits):
    steps = [(i, i + 1) for i in range(127)]
    halo = lax.ppermute(x[T - LOOK :], AXES, steps)
    scale = jnp.repeat(scaling * (math.log2(math.e) / 64), 64)[None, :]
    chosen = pick[:, 0]
    order = jnp.arange(T, dtype=jnp.int32)
    same = chosen[:, None] == chosen[None, :]
    slot_row = jnp.sum((same & (order[:, None] < order[None, :])).astype(jnp.int32), axis=0)
    slot_col = jnp.sum((same & (order[None, :] < order[:, None])).astype(jnp.int32), axis=1)
    place = (chosen >> 1) * (2 * CAP) + (chosen & 1)
    flat_row = (place + 2 * slot_row)[None, :]
    flat_col = (place + 2 * slot_col)[:, None]
    q0, acc0, hid1, rou1 = pl.pallas_call(
        first_kernel,
        out_shape=(shape(LOOK, D), shape(LOOK, 2 * D, dtype=F32), shape(LOOK, D), shape(LOOK, D)),
        scratch_shapes=[pltpu.VMEM((T, D), BF)] * 4 + [pltpu.VMEM((LOOK, D), BF)],
        compiler_params=params(40),
        cost_estimate=cost(4 * 10**9, 8 * MB),
        name="first",
    )(x, triple, mixing, scale)
    valid = jnp.minimum(lax.axis_index(AXES), 1).astype(jnp.int32).reshape(1)
    vmem = pl.BlockSpec(memory_space=pltpu.VMEM)
    buf, hidden, routed = pl.pallas_call(
        second_kernel,
        out_shape=(shape(SLOTS, D), shape(T, D), shape(T, D)),
        in_specs=[pl.BlockSpec(memory_space=pltpu.SMEM)] + [vmem] * 9,
        scratch_shapes=[pltpu.VMEM((LOOK, D), BF)] * 4,
        compiler_params=params(40),
        cost_estimate=cost(2 * 10**9, 8 * MB),
        name="second",
    )(valid, halo, triple, mixing, x, q0, acc0, hid1, rou1, flat_row)
    arrived = lax.all_to_all(buf.reshape(128, CAP, 2, D), AXES, split_axis=0, concat_axis=0, tiled=True)
    chunks = 4
    width = FF // chunks
    out = pl.pallas_call(
        expert_kernel,
        out_shape=shape(SLOTS, D),
        grid=(2, chunks),
        in_specs=[
            pl.BlockSpec((SLOTS, D), lambda e, f: (0, 0)),
            pl.BlockSpec((1, D, width), lambda e, f: (e, 0, f)),
            pl.BlockSpec((1, width, D), lambda e, f: (e, f, 0)),
        ],
        out_specs=pl.BlockSpec((SLOTS, D), lambda e, f: (0, 0)),
        scratch_shapes=[pltpu.VMEM((SLOTS // 2, D), BF), pltpu.VMEM((SLOTS // 2, D), F32), pltpu.VMEM((2, SLOTS // 2, D), BF)],
        compiler_params=params(32),
        cost_estimate=cost(7 * 10**9, 20 * MB),
        name="experts",
    )(arrived.reshape(SLOTS, D), entry, exits)
    back = lax.all_to_all(out.reshape(128, CAP, 2, D), AXES, split_axis=0, concat_axis=0, tiled=True)
    gate = pl.pallas_call(
        gate_kernel,
        out_shape=shape(T, 1, dtype=F32),
        compiler_params=params(16),
        cost_estimate=cost(2 * 10**8, 2 * MB),
        name="gate",
    )(routed, columns, pick)
    return pl.pallas_call(
        last_kernel,
        out_shape=shape(T, D),
        compiler_params=params(24),
        cost_estimate=cost(6 * 10**8, 3 * MB),
        name="last",
    )(back.reshape(SLOTS, D), hidden, gate, flat_col)


def solution(mesh):
    rows = P(AXES, None)
    experts = P(AXES, None, None)
    in_specs = (rows, P(), P(), P(), P(), rows, experts, experts)
    return jax.shard_map(shards, mesh=mesh, in_specs=in_specs, out_specs=rows, check_vma=False)
```

```python
import math

import jax
import jax.numpy as jnp
from jax import lax
from jax.experimental import pallas as pl
from jax.experimental.pallas import tpu as pltpu
from jax.sharding import PartitionSpec as P

D = 768
HEADS = 12
LOOK = 256
T = 512
FF = 3072
CAP = 3
SLOTS = 768
PAIRS = HEADS // 2
LANES = 128
AXES = ("row", "col")
BF = jnp.bfloat16
F32 = jnp.float32
MB = 1 << 20


def dot(a, b):
    return jnp.dot(a, b, preferred_element_type=F32)


def dot_t(a, b):
    return lax.dot_general(a, b, (((1,), (1,)), ((), ())), preferred_element_type=F32)


def norm_rows(value):
    center = value - jnp.mean(value, axis=-1, keepdims=True)
    spread = jnp.mean(center * center, axis=-1, keepdims=True)
    return (center * lax.rsqrt(spread + 1e-05)).astype(BF)


def head_blocks():
    down = lax.shift_right_logical(lax.broadcasted_iota(jnp.int32, (256, 256), 0), 6)
    across = lax.shift_right_logical(lax.broadcasted_iota(jnp.int32, (256, 256), 1), 6)
    return jnp.where(down == across, 1.0, 0.0).astype(BF)


def head_norm(value, blocks):
    square = (value * value).astype(BF)
    return value * lax.rsqrt(dot(square, blocks) * (1.0 / 64) + 1e-06)


def triangles():
    down = lax.broadcasted_iota(jnp.int32, (128, 128), 0)
    across = lax.broadcasted_iota(jnp.int32, (128, 128), 1)
    behind = jnp.where(across >= down, 1.0, 0.0).astype(BF)
    ahead = jnp.where(across <= down, 1.0, 0.0).astype(BF)
    return behind, ahead


def half_lanes(half):
    lane = lax.broadcasted_iota(jnp.int32, (1, LANES), 1)
    mine = (lane < 64) if half == 0 else (lane >= 64)
    return jnp.where(mine, 1.0, 0.0).astype(BF)


def weigh(part):
    return jnp.exp2(part).astype(BF)


def behind_weights(scores, behind):
    top = jnp.concatenate([weigh(scores[:128, :128]) * behind, weigh(scores[:128, 128:])], axis=1)
    low = jnp.concatenate([jnp.zeros((128, 128), BF), weigh(scores[128:, 128:]) * behind], axis=1)
    return jnp.concatenate([top, low], axis=0)


def own_weights(scores, ahead):
    top = jnp.concatenate([weigh(scores[:128, :128]) * ahead, jnp.zeros((128, 128), BF)], axis=1)
    low = jnp.concatenate([weigh(scores[128:, :128]), weigh(scores[128:, 128:]) * ahead], axis=1)
    return jnp.concatenate([top, low], axis=0)


def payload(values, half, ones):
    mask = half_lanes(half)
    return jnp.concatenate([values * mask, ones * mask], axis=1)


def norm_into(source, target, count):
    def step(i, carry):
        r = pl.ds(pl.multiple_of(i * 64, 64), 64)
        target[r, :] = norm_rows(source[r, :].astype(F32))
        return carry

    lax.fori_loop(0, count // 64, step, 0)


def scale_lanes(scale_ref, group):
    lane = lax.broadcasted_iota(jnp.int32, (1, 256), 1)
    value = jnp.full((1, 256), scale_ref[4 * group], F32)
    for h in range(1, 4):
        value = jnp.where(lane >= 64 * h, scale_ref[4 * group + h], value)
    return value * (math.log2(math.e) / 64)


def places(row_ref, flat_out, wide_out, pick_s):
    row = row_ref[...]
    rowf = row.astype(F32)
    rowb = jnp.broadcast_to(rowf, (LANES, T)).astype(BF)
    for r in range(0, T, 128):
        down = lax.broadcasted_iota(jnp.int32, (128, T), 0) + r
        across = lax.broadcasted_iota(jnp.int32, (128, T), 1)
        eye = jnp.where(down == across, 1.0, 0.0).astype(BF)
        wide = dot_t(eye, rowb)
        pick_s[r : r + 128, :] = wide.astype(jnp.int32)
        same = (jnp.concatenate([wide] * 4, axis=1) == rowf) & (across < down)
        same = jnp.where(same, 1.0, 0.0).astype(BF)
        slot = dot(same, jnp.ones((T, LANES), BF)).astype(jnp.int32)
        mine = pick_s[r : r + 128, :]
        wide_out[r : r + 128, :] = (mine >> 1) * (2 * CAP) + (mine & 1) + 2 * slot
        slot_row = dot_t(jnp.ones((8, T), BF), same)[:1].astype(jnp.int32)
        part = row[:, r : r + 128]
        flat_out[:, r : r + 128] = (part >> 1) * (2 * CAP) + (part & 1) + 2 * slot_row


def gates(routed, columns, pick):
    logits = dot(routed, columns)
    lane = lax.broadcasted_iota(jnp.int32, (1, LANES), 1)
    kept = jnp.where(pick == lane, logits[:, :LANES], 0.0) + jnp.where(pick == lane + LANES, logits[:, LANES:], 0.0)
    return 1.0 / (1.0 + jnp.exp(-jnp.sum(kept, axis=1, keepdims=True)))


def finish(ctx, mix_ref, x_ref, x_at, columns_ref, pick_ref, hid_out, rou_out, gate_out):
    for r in range(0, LOOK, 128):
        mixed = dot(ctx[r : r + 128, :], mix_ref[...])
        for s in range(r, r + 128, 32):
            hidden = (x_ref[x_at + s : x_at + s + 32, :].astype(F32) + mixed[s - r : s - r + 32, :]).astype(BF)
            hid_out[s : s + 32, :] = hidden
            rou_out[s : s + 32, :] = norm_rows(hidden.astype(F32))
        gate_out[r : r + 128, :] = gates(rou_out[r : r + 128, :], columns_ref[...], pick_ref[x_at + r : x_at + r + 128, :])


def first_kernel(
    scale_hbm, x_hbm, w_hbm, mix_hbm, columns_hbm, row_hbm,
    q_out, acc_out, hid_out, rou_out, gate_out, flat_out, wide_out, pick_out, x_ref, kv_out, mix_ref, columns_ref,
    normed, wq, q_s, k_s, v_s, ctx, row_ref, scale_ref, sems,
):
    fetch = pltpu.make_async_copy(x_hbm, x_ref, sems.at[0])
    copies = [
        pltpu.make_async_copy(w_hbm.at[:, pl.ds(0, D)], wq, sems.at[1]),
        pltpu.make_async_copy(w_hbm.at[:, pl.ds(D, 2 * D)], kv_out, sems.at[2]),
        pltpu.make_async_copy(columns_hbm, columns_ref, sems.at[3]),
        pltpu.make_async_copy(mix_hbm, mix_ref, sems.at[4]),
        pltpu.make_async_copy(row_hbm, row_ref, sems.at[5]),
        pltpu.make_async_copy(scale_hbm, scale_ref, sems.at[6]),
    ]
    fetch.start()
    for copy in copies:
        copy.start()
    fetch.wait()
    norm_into(x_ref, normed, T)
    for copy in copies:
        copy.wait()
    places(row_ref, flat_out, wide_out, pick_out)
    blocks = head_blocks()
    for g in range(3):
        c = slice(g * 256, g * 256 + 256)
        value = head_norm(dot(normed[...], wq[:, c]), blocks)
        q_s[:, c] = (value * scale_lanes(scale_ref, g)).astype(BF)
        k_s[:, c] = head_norm(dot(normed[...], kv_out[:, c]), blocks).astype(BF)
        v_s[:, c] = dot(normed[...], kv_out[:, D + g * 256 : D + g * 256 + 256]).astype(BF)
    q_out[...] = q_s[:LOOK, :]
    behind, ahead = triangles()
    ones = jnp.ones((LOOK, LANES), BF)
    for pair in range(PAIRS):
        c = slice(pair * LANES, pair * LANES + LANES)
        low = jnp.zeros((LOOK, 256), F32)
        high = jnp.zeros((LOOK, 256), F32)
        for half in range(2):
            mask = half_lanes(half)
            q0 = q_s[:LOOK, c] * mask
            q1 = q_s[LOOK:, c] * mask
            k0 = k_s[:LOOK, c]
            k1 = k_s[LOOK:, c]
            v0 = payload(v_s[:LOOK, c], half, ones)
            v1 = payload(v_s[LOOK:, c], half, ones)
            low += dot(own_weights(dot_t(q0, k0), ahead), v0)
            high += dot(behind_weights(dot_t(q1, k0), behind), v0)
            high += dot(own_weights(dot_t(q1, k1), ahead), v1)
        acc_out[:, pair * 256 : pair * 256 + 256] = low
        ctx[:, c] = (high[:, :LANES] / high[:, LANES:]).astype(BF)
    finish(ctx, mix_ref, x_ref, LOOK, columns_ref, pick_out, hid_out, rou_out, gate_out)


def second_kernel(
    valid_ref, halo_ref, kv_ref, mix_ref, x_ref, columns_ref, q_ref, acc_ref, rou_ref, row_ref, pick_ref,
    buf_out, hid_out, gate_out, normed, k_s, v_s, ctx, routed,
):
    for r in range(0, LOOK, 32):
        normed[r : r + 32, :] = norm_rows(halo_ref[r : r + 32, :].astype(F32))
    blocks = head_blocks()
    for g in range(3):
        c = slice(g * 256, g * 256 + 256)
        k_s[:, c] = head_norm(dot(normed[...], kv_ref[:, c]), blocks).astype(BF)
        v_s[:, c] = dot(normed[...], kv_ref[:, D + g * 256 : D + g * 256 + 256]).astype(BF)
    behind, _ = triangles()
    ones = jnp.full((LOOK, LANES), valid_ref[0].astype(F32)).astype(BF)
    for pair in range(PAIRS):
        c = slice(pair * LANES, pair * LANES + LANES)
        low = acc_ref[:, pair * 256 : pair * 256 + 256]
        for half in range(2):
            q0 = q_ref[:, c] * half_lanes(half)
            low += dot(behind_weights(dot_t(q0, k_s[:, c]), behind), payload(v_s[:, c] * ones, half, ones))
        ctx[:, c] = (low[:, :LANES] / low[:, LANES:]).astype(BF)
    finish(ctx, mix_ref, x_ref, 0, columns_ref, pick_ref, hid_out, routed, gate_out)
    for s in range(0, SLOTS, 256):
        place = lax.broadcasted_iota(jnp.int32, (256, T), 0) + s
        pick = jnp.where(place == row_ref[...], 1.0, 0.0).astype(BF)
        rows = dot(pick[:, :LOOK], routed[...]) + dot(pick[:, LOOK:], rou_ref[...])
        buf_out[s // 2 : s // 2 + 128] = rows.astype(BF).reshape(128, 2, D)


def take_rows(expert):
    down = lax.broadcasted_iota(jnp.int32, (128, 256), 0)
    across = lax.broadcasted_iota(jnp.int32, (128, 256), 1)
    return jnp.where(across == 2 * down + expert, 1.0, 0.0).astype(BF)


def put_rows(expert):
    down = lax.broadcasted_iota(jnp.int32, (256, 128), 0)
    across = lax.broadcasted_iota(jnp.int32, (256, 128), 1)
    return jnp.where(down == 2 * across + expert, 1.0, 0.0).astype(BF)


def expert_kernel(in_ref, first_ref, second_ref, out_ref, rows, hidden, done):
    arrived = in_ref[...].reshape(SLOTS, D)
    for e in range(2):
        pick = take_rows(e)
        for b in range(3):
            rows[e, b * 128 : b * 128 + 128, :] = dot(pick, arrived[b * 256 : b * 256 + 256, :]).astype(BF)
    for e in range(2):
        for s in range(0, FF, 768):
            hidden[:, s : s + 768] = jnp.maximum(dot(rows[e], first_ref[e, :, s : s + 768]), 0.0).astype(BF)
        done[e] = dot(hidden[...], second_ref[e]).astype(BF)
    for b in range(3):
        r = slice(b * 128, b * 128 + 128)
        mixed = dot(put_rows(0), done[0, r, :]) + dot(put_rows(1), done[1, r, :])
        out_ref[r] = mixed.astype(BF).reshape(128, 2, D)


def last_kernel(back_ref, hid0_ref, hid1_ref, gate0_ref, gate1_ref, wide_ref, out_ref):
    back = back_ref[...].reshape(SLOTS, D)
    for r, hid_ref, gate_ref in ((0, hid0_ref, gate0_ref), (LOOK, hid1_ref, gate1_ref)):
        across = lax.broadcasted_iota(jnp.int32, (LOOK, SLOTS), 1)
        place = jnp.concatenate([wide_ref[r : r + LOOK, :]] * 6, axis=1)
        pick = jnp.where(across == place, 1.0, 0.0).astype(BF)
        picked = dot(pick, back)
        out_ref[r : r + LOOK, :] = (hid_ref[...].astype(F32) + gate_ref[...] * picked).astype(BF)


def params(limit):
    return pltpu.CompilerParams(vmem_limit_bytes=limit * MB)


def shape(*dims, dtype=BF):
    return jax.ShapeDtypeStruct(dims, dtype)


def cost(flops, moved, exps=0):
    return pl.CostEstimate(flops=flops, bytes_accessed=moved, transcendentals=exps)


def far(value):
    return pltpu.with_memory_space_constraint(value, pltpu.HBM)


def shards(x, triple, mixing, scaling, columns, pick, entry, exits):
    steps = [(i, i + 1) for i in range(127)]
    halo = lax.ppermute(x[T - LOOK :], AXES, steps)
    row = pick.reshape(1, T)
    vmem = pl.BlockSpec(memory_space=pltpu.VMEM)
    smem = pl.BlockSpec(memory_space=pltpu.SMEM)
    hbm = pl.BlockSpec(memory_space=pltpu.HBM)
    q0, acc0, hid1, rou1, gate1, flat, wide, chosen, x_near, kv, mix_near, columns_near = pl.pallas_call(
        first_kernel,
        out_shape=(
            shape(LOOK, D),
            shape(LOOK, 2 * D, dtype=F32),
            shape(LOOK, D),
            shape(LOOK, D),
            shape(LOOK, 1, dtype=F32),
            shape(1, T, dtype=jnp.int32),
            shape(T, LANES, dtype=jnp.int32),
            shape(T, LANES, dtype=jnp.int32),
            shape(T, D),
            shape(D, 2 * D),
            shape(D, D),
            shape(D, 256),
        ),
        in_specs=[hbm] * 6,
        out_specs=(vmem,) * 12,
        scratch_shapes=[pltpu.VMEM((T, D), BF), pltpu.VMEM((D, D), BF)]
        + [pltpu.VMEM((T, D), BF)] * 3
        + [
            pltpu.VMEM((LOOK, D), BF),
            pltpu.VMEM((1, T), jnp.int32),
            pltpu.SMEM((HEADS,), F32),
            pltpu.SemaphoreType.DMA((7,)),
        ],
        compiler_params=params(16),
        cost_estimate=cost(4 * 10**9, 8 * MB),
        name="first",
    )(*(far(a) for a in (scaling, x, triple, mixing, columns, row)))
    valid = jnp.minimum(lax.axis_index(AXES), 1).astype(jnp.int32).reshape(1)
    buf, hid0, gate0 = pl.pallas_call(
        second_kernel,
        out_shape=(shape(SLOTS // 2, 2, D), shape(LOOK, D), shape(LOOK, 1, dtype=F32)),
        in_specs=[smem] + [vmem] * 10,
        out_specs=(vmem,) * 3,
        scratch_shapes=[pltpu.VMEM((LOOK, D), BF)] * 5,
        compiler_params=params(16),
        cost_estimate=cost(2 * 10**9, 8 * MB),
        name="second",
    )(valid, halo, kv, mix_near, x_near, columns_near, q0, acc0, rou1, flat, chosen)
    arrived = lax.all_to_all(buf.reshape(128, CAP, 2, D), AXES, split_axis=0, concat_axis=0, tiled=True)
    out = pl.pallas_call(
        expert_kernel,
        out_shape=shape(SLOTS // 2, 2, D),
        scratch_shapes=[pltpu.VMEM((2, SLOTS // 2, D), BF), pltpu.VMEM((SLOTS // 2, FF), BF), pltpu.VMEM((2, SLOTS // 2, D), BF)],
        compiler_params=params(14),
        cost_estimate=cost(7 * 10**9, 20 * MB),
        name="experts",
    )(arrived.reshape(SLOTS // 2, 2, D), entry, exits)
    back = lax.all_to_all(out.reshape(128, CAP, 2, D), AXES, split_axis=0, concat_axis=0, tiled=True)
    return pl.pallas_call(
        last_kernel,
        out_shape=shape(T, D),
        compiler_params=params(16),
        cost_estimate=cost(6 * 10**8, 3 * MB),
        name="last",
    )(back.reshape(SLOTS // 2, 2, D), hid0, hid1, gate0, gate1, wide)


def solution(mesh):
    rows = P(AXES, None)
    experts = P(AXES, None, None)
    in_specs = (rows, P(), P(), P(), P(), rows, experts, experts)
    return jax.shard_map(shards, mesh=mesh, in_specs=in_specs, out_specs=rows, check_vma=False)
```

```python
import math

import jax
import jax.numpy as jnp
from jax import lax
from jax.experimental import pallas as pl
from jax.experimental.pallas import tpu as pltpu
from jax.sharding import PartitionSpec as P

D = 768
HEADS = 12
LOOK = 256
T = 512
FF = 3072
CAP = 3
SLOTS = 768
PAIRS = HEADS // 2
LANES = 128
AXES = ("row", "col")
BF = jnp.bfloat16
F32 = jnp.float32
MB = 1 << 20


def dot(a, b):
    return jnp.dot(a, b, preferred_element_type=F32)


def dot_t(a, b):
    return lax.dot_general(a, b, (((1,), (1,)), ((), ())), preferred_element_type=F32)


def norm_rows(value):
    center = value - jnp.mean(value, axis=-1, keepdims=True)
    spread = jnp.mean(center * center, axis=-1, keepdims=True)
    return (center * lax.rsqrt(spread + 1e-05)).astype(BF)


def head_blocks():
    down = lax.shift_right_logical(lax.broadcasted_iota(jnp.int32, (256, 256), 0), 6)
    across = lax.shift_right_logical(lax.broadcasted_iota(jnp.int32, (256, 256), 1), 6)
    return jnp.where(down == across, 1.0, 0.0).astype(BF)


def head_norm(value, blocks):
    square = (value * value).astype(BF)
    return value * lax.rsqrt(dot(square, blocks) * (1.0 / 64) + 1e-06)


def triangles():
    down = lax.broadcasted_iota(jnp.int32, (128, 128), 0)
    across = lax.broadcasted_iota(jnp.int32, (128, 128), 1)
    behind = jnp.where(across >= down, 1.0, 0.0).astype(BF)
    ahead = jnp.where(across <= down, 1.0, 0.0).astype(BF)
    return behind, ahead


def half_lanes(half):
    lane = lax.broadcasted_iota(jnp.int32, (1, LANES), 1)
    mine = (lane < 64) if half == 0 else (lane >= 64)
    return jnp.where(mine, 1.0, 0.0).astype(BF)


def weigh(part):
    return jnp.exp2(part).astype(BF)


def behind_weights(scores, behind):
    top = jnp.concatenate([weigh(scores[:128, :128]) * behind, weigh(scores[:128, 128:])], axis=1)
    low = jnp.concatenate([jnp.zeros((128, 128), BF), weigh(scores[128:, 128:]) * behind], axis=1)
    return jnp.concatenate([top, low], axis=0)


def own_weights(scores, ahead):
    top = jnp.concatenate([weigh(scores[:128, :128]) * ahead, jnp.zeros((128, 128), BF)], axis=1)
    low = jnp.concatenate([weigh(scores[128:, :128]), weigh(scores[128:, 128:]) * ahead], axis=1)
    return jnp.concatenate([top, low], axis=0)


def payload(values, half, ones):
    mask = half_lanes(half)
    return jnp.concatenate([values * mask, ones * mask], axis=1)


def norm_into(source, target, count):
    def step(i, carry):
        r = pl.ds(pl.multiple_of(i * 64, 64), 64)
        target[r, :] = norm_rows(source[r, :].astype(F32))
        return carry

    lax.fori_loop(0, count // 64, step, 0)


def scale_lanes(scale_ref, group):
    lane = lax.broadcasted_iota(jnp.int32, (1, 256), 1)
    value = jnp.full((1, 256), scale_ref[4 * group], F32)
    for h in range(1, 4):
        value = jnp.where(lane >= 64 * h, scale_ref[4 * group + h], value)
    return value * (math.log2(math.e) / 64)


def places(row_ref, flat_out, wide_out):
    row = row_ref[...]
    rowf = row.astype(F32)
    rowb = jnp.broadcast_to(rowf, (LANES, T)).astype(BF)
    for r in range(0, T, 128):
        down = lax.broadcasted_iota(jnp.int32, (128, T), 0) + r
        across = lax.broadcasted_iota(jnp.int32, (128, T), 1)
        eye = jnp.where(down == across, 1.0, 0.0).astype(BF)
        wide = dot_t(eye, rowb)
        same = (jnp.concatenate([wide] * 4, axis=1) == rowf) & (across < down)
        same = jnp.where(same, 1.0, 0.0).astype(BF)
        slot = dot(same, jnp.ones((T, LANES), BF)).astype(jnp.int32)
        mine = wide.astype(jnp.int32)
        wide_out[r : r + 128, :] = (mine >> 1) * (2 * CAP) + (mine & 1) + 2 * slot
        slot_row = dot_t(jnp.ones((8, T), BF), same)[:1].astype(jnp.int32)
        part = row[:, r : r + 128]
        flat_out[:, r : r + 128] = (part >> 1) * (2 * CAP) + (part & 1) + 2 * slot_row


def device_index():
    return lax.axis_index("row") * lax.axis_size("col") + lax.axis_index("col")


def own_columns(columns):
    down = lax.broadcasted_iota(jnp.int32, (256, 256), 0)
    across = lax.broadcasted_iota(jnp.int32, (256, 256), 1)
    pick = jnp.where(down == 2 * device_index() + (across >> 7), 1.0, 0.0).astype(BF)
    return dot(columns, pick).astype(BF)


def finish(ctx, mix_ref, x_ref, x_at, hid_out, rou_out):
    for r in range(0, LOOK, 128):
        mixed = dot(ctx[r : r + 128, :], mix_ref[...])
        for s in range(r, r + 128, 32):
            hidden = (x_ref[x_at + s : x_at + s + 32, :].astype(F32) + mixed[s - r : s - r + 32, :]).astype(BF)
            hid_out[s : s + 32, :] = hidden
            rou_out[s : s + 32, :] = norm_rows(hidden.astype(F32))


def dispatch(flat, at, routed):
    place = lax.broadcasted_iota(jnp.int32, (256, LOOK), 0) + at
    return dot(jnp.where(place == flat, 1.0, 0.0).astype(BF), routed[...]).astype(BF)


def wait_last(copies):
    def step(i, carry):
        for copy in copies:
            copy.wait()
        return carry

    lax.fori_loop(0, jnp.minimum(device_index(), 0) + 1, step, 0)


def first_kernel(
    scale_hbm, x_hbm, w_hbm, mix_hbm, columns_hbm, row_hbm, entry_hbm, exits_hbm,
    q_out, acc_out, hid_out, buf_out, flat_out, wide_out, x_ref, kv_out, mix_ref, columns_out, entry_out, exit_out,
    normed, wq, q_s, k_s, v_s, ctx, routed, columns_ref, row_ref, scale_ref, sems, far_sems,
):
    fetch = pltpu.make_async_copy(x_hbm, x_ref, sems.at[0])
    copies = [
        pltpu.make_async_copy(w_hbm.at[:, pl.ds(0, D)], wq, sems.at[1]),
        pltpu.make_async_copy(w_hbm.at[:, pl.ds(D, 2 * D)], kv_out, sems.at[2]),
        pltpu.make_async_copy(columns_hbm, columns_ref, sems.at[3]),
        pltpu.make_async_copy(mix_hbm, mix_ref, sems.at[4]),
        pltpu.make_async_copy(row_hbm, row_ref, sems.at[5]),
        pltpu.make_async_copy(scale_hbm, scale_ref, sems.at[6]),
    ]
    fetch.start()
    for copy in copies:
        copy.start()
    fetch.wait()
    norm_into(x_ref, normed, T)
    for copy in copies:
        copy.wait()
    later = [
        pltpu.make_async_copy(entry_hbm, entry_out, far_sems.at[0]),
        pltpu.make_async_copy(exits_hbm.at[0], exit_out, far_sems.at[1]),
    ]
    for copy in later:
        copy.start()
    places(row_ref, flat_out, wide_out)
    columns_out[...] = own_columns(columns_ref[...])
    blocks = head_blocks()
    for g in range(3):
        c = slice(g * 256, g * 256 + 256)
        value = head_norm(dot(normed[...], wq[:, c]), blocks)
        q_s[:, c] = (value * scale_lanes(scale_ref, g)).astype(BF)
        k_s[:, c] = head_norm(dot(normed[...], kv_out[:, c]), blocks).astype(BF)
        v_s[:, c] = dot(normed[...], kv_out[:, D + g * 256 : D + g * 256 + 256]).astype(BF)
    q_out[...] = q_s[:LOOK, :]
    behind, ahead = triangles()
    ones = jnp.ones((LOOK, LANES), BF)
    for pair in range(PAIRS):
        c = slice(pair * LANES, pair * LANES + LANES)
        low = jnp.zeros((LOOK, 256), F32)
        high = jnp.zeros((LOOK, 256), F32)
        for half in range(2):
            mask = half_lanes(half)
            q0 = q_s[:LOOK, c] * mask
            q1 = q_s[LOOK:, c] * mask
            k0 = k_s[:LOOK, c]
            k1 = k_s[LOOK:, c]
            v0 = payload(v_s[:LOOK, c], half, ones)
            v1 = payload(v_s[LOOK:, c], half, ones)
            low += dot(own_weights(dot_t(q0, k0), ahead), v0)
            high += dot(behind_weights(dot_t(q1, k0), behind), v0)
            high += dot(own_weights(dot_t(q1, k1), ahead), v1)
        acc_out[:, pair * 256 : pair * 256 + 256] = low
        ctx[:, c] = (high[:, :LANES] / high[:, LANES:]).astype(BF)
    finish(ctx, mix_ref, x_ref, LOOK, hid_out, routed)
    for s in range(0, SLOTS, 256):
        buf_out[s : s + 256, :] = dispatch(flat_out[:, LOOK:], s, routed)
    wait_last(later)


def second_kernel(
    halo_ref, kv_ref, mix_ref, x_ref, q_ref, acc_ref, buf_ref, flat_ref, exits_hbm,
    buf_out, hid_out, exit_out, normed, k_s, v_s, ctx, routed, far_sem,
):
    later = pltpu.make_async_copy(exits_hbm.at[1], exit_out, far_sem)
    later.start()
    for r in range(0, LOOK, 32):
        normed[r : r + 32, :] = norm_rows(halo_ref[r : r + 32, :].astype(F32))
    blocks = head_blocks()
    for g in range(3):
        c = slice(g * 256, g * 256 + 256)
        k_s[:, c] = head_norm(dot(normed[...], kv_ref[:, c]), blocks).astype(BF)
        v_s[:, c] = dot(normed[...], kv_ref[:, D + g * 256 : D + g * 256 + 256]).astype(BF)
    behind, _ = triangles()
    ones = jnp.full((LOOK, LANES), jnp.minimum(device_index(), 1).astype(F32)).astype(BF)
    for pair in range(PAIRS):
        c = slice(pair * LANES, pair * LANES + LANES)
        low = acc_ref[:, pair * 256 : pair * 256 + 256]
        for half in range(2):
            q0 = q_ref[:, c] * half_lanes(half)
            low += dot(behind_weights(dot_t(q0, k_s[:, c]), behind), payload(v_s[:, c] * ones, half, ones))
        ctx[:, c] = (low[:, :LANES] / low[:, LANES:]).astype(BF)
    finish(ctx, mix_ref, x_ref, 0, hid_out, routed)
    for s in range(0, SLOTS, 256):
        rows = dispatch(flat_ref[:, :LOOK], s, routed) + buf_ref[s : s + 256, :]
        buf_out[s // 2 : s // 2 + 128] = rows.reshape(128, 2, D)
    wait_last([later])


def by_expert(back):
    down = lax.broadcasted_iota(jnp.int32, (256, 256), 0)
    across = lax.broadcasted_iota(jnp.int32, (256, 256), 1)
    if back:
        down, across = across, down
    return jnp.where(across == 2 * (down & 127) + (down >> 7), 1.0, 0.0).astype(BF)


def expert_kernel(in_ref, columns_ref, first_ref, exit0_ref, exit1_ref, out_ref, rows, hidden, done):
    order = by_expert(False)
    for b in range(3):
        both = dot(order, in_ref[b * 128 : b * 128 + 128].reshape(256, D)).astype(BF)
        rows[0, b * 128 : b * 128 + 128, :] = both[:128]
        rows[1, b * 128 : b * 128 + 128, :] = both[128:]
    for e in range(2):
        logit = dot(rows[e], columns_ref[:, e * LANES : e * LANES + LANES])
        gate = jnp.concatenate([1.0 / (1.0 + jnp.exp(-logit))] * 2, axis=1)
        for s in range(0, FF, 768):
            hidden[:, s : s + 768] = jnp.maximum(dot(rows[e], first_ref[e, :, s : s + 768]), 0.0).astype(BF)
        for s in range(0, D, 256):
            done[e, :, s : s + 256] = (gate * dot(hidden[...], (exit0_ref, exit1_ref)[e][:, s : s + 256])).astype(BF)
    order = by_expert(True)
    for b in range(3):
        r = slice(b * 128, b * 128 + 128)
        both = jnp.concatenate([done[0, r, :], done[1, r, :]], axis=0)
        out_ref[r] = dot(order, both).astype(BF).reshape(128, 2, D)


def last_kernel(back_ref, hid0_ref, hid1_ref, wide_ref, out_ref):
    back = back_ref[...].reshape(SLOTS, D)
    for r, hid_ref in ((0, hid0_ref), (LOOK, hid1_ref)):
        across = lax.broadcasted_iota(jnp.int32, (LOOK, SLOTS), 1)
        place = jnp.concatenate([wide_ref[r : r + LOOK, :]] * 6, axis=1)
        pick = jnp.where(across == place, 1.0, 0.0).astype(BF)
        out_ref[r : r + LOOK, :] = (hid_ref[...].astype(F32) + dot(pick, back)).astype(BF)


def params(limit):
    return pltpu.CompilerParams(vmem_limit_bytes=limit * MB)


def shape(*dims, dtype=BF):
    return jax.ShapeDtypeStruct(dims, dtype)


def cost(flops, moved, exps=0):
    return pl.CostEstimate(flops=flops, bytes_accessed=moved, transcendentals=exps)


def far(value):
    return pltpu.with_memory_space_constraint(value, pltpu.HBM)


VM = pl.BlockSpec(memory_space=pltpu.VMEM)
HB = pl.BlockSpec(memory_space=pltpu.HBM)


def call_first(scaling, x, triple, mixing, columns, row, entry, exits):
    return pl.pallas_call(
        first_kernel,
        out_shape=(
            shape(LOOK, D),
            shape(LOOK, 2 * D, dtype=F32),
            shape(LOOK, D),
            shape(SLOTS, D),
            shape(1, T, dtype=jnp.int32),
            shape(T, LANES, dtype=jnp.int32),
            shape(T, D),
            shape(D, 2 * D),
            shape(D, D),
            shape(D, 256),
            shape(2, D, FF),
            shape(FF, D),
        ),
        in_specs=[HB] * 8,
        out_specs=(VM,) * 12,
        scratch_shapes=[pltpu.VMEM((T, D), BF), pltpu.VMEM((D, D), BF)]
        + [pltpu.VMEM((T, D), BF)] * 3
        + [
            pltpu.VMEM((LOOK, D), BF),
            pltpu.VMEM((LOOK, D), BF),
            pltpu.VMEM((D, 256), BF),
            pltpu.VMEM((1, T), jnp.int32),
            pltpu.SMEM((HEADS,), F32),
            pltpu.SemaphoreType.DMA((7,)),
            pltpu.SemaphoreType.DMA((2,)),
        ],
        compiler_params=params(16),
        cost_estimate=cost(4 * 10**9, 8 * MB),
        name="first",
    )(*(far(a) for a in (scaling, x, triple, mixing, columns, row, entry, exits)))


def call_second(halo, kv, mixing, x, q0, acc0, buf1, flat, exits):
    return pl.pallas_call(
        second_kernel,
        out_shape=(shape(SLOTS // 2, 2, D), shape(LOOK, D), shape(FF, D)),
        in_specs=[VM] * 8 + [HB],
        out_specs=(VM,) * 3,
        scratch_shapes=[pltpu.VMEM((LOOK, D), BF)] * 5 + [pltpu.SemaphoreType.DMA],
        compiler_params=params(16),
        cost_estimate=cost(2 * 10**9, 8 * MB),
        name="second",
    )(halo, kv, mixing, x, q0, acc0, buf1, flat, far(exits))


def call_experts(arrived, columns, entry, exit0, exit1):
    return pl.pallas_call(
        expert_kernel,
        out_shape=shape(SLOTS // 2, 2, D),
        scratch_shapes=[
            pltpu.VMEM((2, SLOTS // 2, D), BF),
            pltpu.VMEM((SLOTS // 2, FF), BF),
            pltpu.VMEM((2, SLOTS // 2, D), BF),
        ],
        compiler_params=params(14),
        cost_estimate=cost(7 * 10**9, 20 * MB),
        name="experts",
    )(arrived, columns, entry, exit0, exit1)


def call_last(back, hid0, hid1, wide):
    return pl.pallas_call(
        last_kernel,
        out_shape=shape(T, D),
        compiler_params=params(16),
        cost_estimate=cost(6 * 10**8, 3 * MB),
        name="last",
    )(back, hid0, hid1, wide)


def exchange(rows):
    rows = rows.reshape(128, CAP, 2, D)
    return lax.all_to_all(rows, AXES, split_axis=0, concat_axis=0, tiled=True).reshape(SLOTS // 2, 2, D)


def shards(x, triple, mixing, scaling, columns, pick, entry, exits):
    halo = lax.ppermute(x[T - LOOK :], AXES, [(i, i + 1) for i in range(127)])
    first = call_first(scaling, x, triple, mixing, columns, pick.reshape(1, T), entry, exits)
    q0, acc0, hid1, buf1, flat, wide, x_near, kv, mix_near, columns_near, entry_near, exit0 = first
    buf, hid0, exit1 = call_second(halo, kv, mix_near, x_near, q0, acc0, buf1, flat, exits)
    back = exchange(call_experts(exchange(buf), columns_near, entry_near, exit0, exit1))
    return call_last(back, hid0, hid1, wide)


def solution(mesh):
    rows = P(AXES, None)
    experts = P(AXES, None, None)
    in_specs = (rows, P(), P(), P(), P(), rows, experts, experts)
    return jax.shard_map(shards, mesh=mesh, in_specs=in_specs, out_specs=rows, check_vma=False)
```

```python
import math

import jax
import jax.numpy as jnp
from jax import lax
from jax.experimental import pallas as pl
from jax.experimental.pallas import tpu as pltpu
from jax.sharding import PartitionSpec as P

D = 768
HEADS = 12
LOOK = 256
T = 512
FF = 3072
CAP = 3
SLOTS = 768
PAIRS = HEADS // 2
LANES = 128
AXES = ("row", "col")
BF = jnp.bfloat16
F32 = jnp.float32
MB = 1 << 20


def dot(a, b):
    return jnp.dot(a, b, preferred_element_type=F32)


def dot_t(a, b):
    return lax.dot_general(a, b, (((1,), (1,)), ((), ())), preferred_element_type=F32)


def norm_rows(value):
    center = value - jnp.mean(value, axis=-1, keepdims=True)
    spread = jnp.mean(center * center, axis=-1, keepdims=True)
    return (center * lax.rsqrt(spread + 1e-05)).astype(BF)


def head_blocks():
    down = lax.shift_right_logical(lax.broadcasted_iota(jnp.int32, (256, 256), 0), 6)
    across = lax.shift_right_logical(lax.broadcasted_iota(jnp.int32, (256, 256), 1), 6)
    return jnp.where(down == across, 1.0, 0.0).astype(BF)


def head_norm(value, blocks):
    square = (value * value).astype(BF)
    return value * lax.rsqrt(dot(square, blocks) * (1.0 / 64) + 1e-06)


def triangles():
    down = lax.broadcasted_iota(jnp.int32, (128, 128), 0)
    across = lax.broadcasted_iota(jnp.int32, (128, 128), 1)
    behind = jnp.where(across >= down, 1.0, 0.0).astype(BF)
    ahead = jnp.where(across <= down, 1.0, 0.0).astype(BF)
    return behind, ahead


def half_lanes(half):
    lane = lax.broadcasted_iota(jnp.int32, (1, LANES), 1)
    mine = (lane < 64) if half == 0 else (lane >= 64)
    return jnp.where(mine, 1.0, 0.0).astype(BF)


def weigh(part):
    return jnp.exp2(part).astype(BF)


def behind_weights(scores, behind):
    top = jnp.concatenate([weigh(scores[:128, :128]) * behind, weigh(scores[:128, 128:])], axis=1)
    low = jnp.concatenate([jnp.zeros((128, 128), BF), weigh(scores[128:, 128:]) * behind], axis=1)
    return jnp.concatenate([top, low], axis=0)


def own_weights(scores, ahead):
    top = jnp.concatenate([weigh(scores[:128, :128]) * ahead, jnp.zeros((128, 128), BF)], axis=1)
    low = jnp.concatenate([weigh(scores[128:, :128]), weigh(scores[128:, 128:]) * ahead], axis=1)
    return jnp.concatenate([top, low], axis=0)


def payload(values, half, ones):
    mask = half_lanes(half)
    return jnp.concatenate([values * mask, ones * mask], axis=1)


def norm_into(source, target, count):
    def step(i, carry):
        r = pl.ds(pl.multiple_of(i * 64, 64), 64)
        target[r, :] = norm_rows(source[r, :].astype(F32))
        return carry

    lax.fori_loop(0, count // 64, step, 0)


def scale_lanes(scale_ref, group):
    lane = lax.broadcasted_iota(jnp.int32, (1, 256), 1)
    value = jnp.full((1, 256), scale_ref[4 * group], F32)
    for h in range(1, 4):
        value = jnp.where(lane >= 64 * h, scale_ref[4 * group + h], value)
    return value * (math.log2(math.e) / 64)


def places(row_ref, flat_out, wide_out):
    row = row_ref[...]
    rowf = row.astype(F32)
    rowb = jnp.broadcast_to(rowf, (LANES, T)).astype(BF)
    for r in range(0, T, 128):
        down = lax.broadcasted_iota(jnp.int32, (128, T), 0) + r
        across = lax.broadcasted_iota(jnp.int32, (128, T), 1)
        eye = jnp.where(down == across, 1.0, 0.0).astype(BF)
        wide = dot_t(eye, rowb)
        same = (jnp.concatenate([wide] * 4, axis=1) == rowf) & (across < down)
        same = jnp.where(same, 1.0, 0.0).astype(BF)
        slot = dot(same, jnp.ones((T, LANES), BF)).astype(jnp.int32)
        mine = wide.astype(jnp.int32)
        wide_out[r : r + 128, :] = (mine >> 1) * (2 * CAP) + (mine & 1) + 2 * slot
        slot_row = dot_t(jnp.ones((8, T), BF), same)[:1].astype(jnp.int32)
        part = row[:, r : r + 128]
        flat_out[:, r : r + 128] = (part >> 1) * (2 * CAP) + (part & 1) + 2 * slot_row


def device_index():
    return lax.axis_index("row") * lax.axis_size("col") + lax.axis_index("col")


def own_columns(columns):
    down = lax.broadcasted_iota(jnp.int32, (256, 256), 0)
    across = lax.broadcasted_iota(jnp.int32, (256, 256), 1)
    pick = jnp.where(down == 2 * device_index() + (across >> 7), 1.0, 0.0).astype(BF)
    return dot(columns, pick).astype(BF)


def finish(ctx, mix_ref, x_ref, hid_out, rou_out):
    for r in range(0, LOOK, 128):
        mixed = dot(ctx[r : r + 128, :], mix_ref[...])
        for s in range(r, r + 128, 32):
            hidden = (x_ref[s : s + 32, :].astype(F32) + mixed[s - r : s - r + 32, :]).astype(BF)
            hid_out[s : s + 32, :] = hidden
            rou_out[s : s + 32, :] = norm_rows(hidden.astype(F32))


def dispatch(flat, at, routed):
    place = lax.broadcasted_iota(jnp.int32, (256, LOOK), 0) + at
    return dot(jnp.where(place == flat, 1.0, 0.0).astype(BF), routed[...]).astype(BF)


def apart(work):
    def step(i, carry):
        work()
        return carry

    lax.fori_loop(0, jnp.minimum(device_index(), 0) + 1, step, 0)


def load_kernel(x_hbm, low_out, high_out, normed_out, sems):
    high = pltpu.make_async_copy(x_hbm.at[pl.ds(LOOK, LOOK), :], high_out, sems.at[0])
    low = pltpu.make_async_copy(x_hbm.at[pl.ds(0, LOOK), :], low_out, sems.at[1])
    high.start()
    low.start()
    high.wait()
    low.wait()
    for r in range(0, LOOK, 32):
        normed_out[r : r + 32, :] = norm_rows(high_out[r : r + 32, :].astype(F32))


def first_kernel(
    low_ref, high_ref, normed_ref, scale_hbm, w_hbm, mix_hbm, columns_hbm, row_hbm,
    q_out, acc_out, hid_out, buf_out, flat_out, wide_out, kv_out, mix_ref, columns_out,
    normed, wq, q_s, k_s, v_s, ctx, routed, columns_ref, row_ref, scale_ref, sems,
):
    early = [
        pltpu.make_async_copy(row_hbm, row_ref, sems.at[5]),
        pltpu.make_async_copy(columns_hbm, columns_ref, sems.at[3]),
    ]
    dense = [
        pltpu.make_async_copy(w_hbm.at[:, pl.ds(0, D)], wq, sems.at[1]),
        pltpu.make_async_copy(w_hbm.at[:, pl.ds(D, 2 * D)], kv_out, sems.at[2]),
        pltpu.make_async_copy(scale_hbm, scale_ref, sems.at[6]),
    ]
    mix = [pltpu.make_async_copy(mix_hbm, mix_ref, sems.at[4])]
    for copy in early + dense + mix:
        copy.start()
    for copy in early:
        copy.wait()

    def prepare():
        for r in range(0, LOOK, 32):
            normed[r : r + 32, :] = norm_rows(low_ref[r : r + 32, :].astype(F32))
        normed[LOOK:, :] = normed_ref[...]
        places(row_ref, flat_out, wide_out)
        columns_out[...] = own_columns(columns_ref[...])

    apart(prepare)
    for copy in dense:
        copy.wait()
    blocks = head_blocks()
    for g in range(3):
        c = slice(g * 256, g * 256 + 256)
        value = head_norm(dot(normed[...], wq[:, c]), blocks)
        q_s[:, c] = (value * scale_lanes(scale_ref, g)).astype(BF)
        k_s[:, c] = head_norm(dot(normed[...], kv_out[:, c]), blocks).astype(BF)
        v_s[:, c] = dot(normed[...], kv_out[:, D + g * 256 : D + g * 256 + 256]).astype(BF)
    q_out[...] = q_s[:LOOK, :]
    behind, ahead = triangles()
    ones = jnp.ones((LOOK, LANES), BF)
    for pair in range(PAIRS):
        c = slice(pair * LANES, pair * LANES + LANES)
        low = jnp.zeros((LOOK, 256), F32)
        high = jnp.zeros((LOOK, 256), F32)
        for half in range(2):
            mask = half_lanes(half)
            q0 = q_s[:LOOK, c] * mask
            q1 = q_s[LOOK:, c] * mask
            k0 = k_s[:LOOK, c]
            k1 = k_s[LOOK:, c]
            v0 = payload(v_s[:LOOK, c], half, ones)
            v1 = payload(v_s[LOOK:, c], half, ones)
            low += dot(own_weights(dot_t(q0, k0), ahead), v0)
            high += dot(behind_weights(dot_t(q1, k0), behind), v0)
            high += dot(own_weights(dot_t(q1, k1), ahead), v1)
        acc_out[:, pair * 256 : pair * 256 + 256] = low
        ctx[:, c] = (high[:, :LANES] / high[:, LANES:]).astype(BF)
    apart(mix[0].wait)
    finish(ctx, mix_ref, high_ref, hid_out, routed)
    for s in range(0, SLOTS, 256):
        buf_out[s : s + 256, :] = dispatch(flat_out[:, LOOK:], s, routed)


def second_kernel(
    halo_ref, kv_ref, mix_ref, x_ref, q_ref, acc_ref, buf_ref, flat_ref,
    buf_out, hid_out, k_s, v_s, ctx, routed,
):
    blocks = head_blocks()
    for g in range(3):
        c = slice(g * 256, g * 256 + 256)
        k_s[:, c] = head_norm(dot(halo_ref[...], kv_ref[:, c]), blocks).astype(BF)
        v_s[:, c] = dot(halo_ref[...], kv_ref[:, D + g * 256 : D + g * 256 + 256]).astype(BF)
    behind, _ = triangles()
    ones = jnp.full((LOOK, LANES), jnp.minimum(device_index(), 1).astype(F32)).astype(BF)
    for pair in range(PAIRS):
        c = slice(pair * LANES, pair * LANES + LANES)
        low = acc_ref[:, pair * 256 : pair * 256 + 256]
        for half in range(2):
            q0 = q_ref[:, c] * half_lanes(half)
            low += dot(behind_weights(dot_t(q0, k_s[:, c]), behind), payload(v_s[:, c] * ones, half, ones))
        ctx[:, c] = (low[:, :LANES] / low[:, LANES:]).astype(BF)
    finish(ctx, mix_ref, x_ref, hid_out, routed)
    for s in range(0, SLOTS, 256):
        rows = dispatch(flat_ref[:, :LOOK], s, routed) + buf_ref[s : s + 256, :]
        buf_out[s // 2 : s // 2 + 128] = rows.reshape(128, 2, D)


def by_expert(back):
    down = lax.broadcasted_iota(jnp.int32, (256, 256), 0)
    across = lax.broadcasted_iota(jnp.int32, (256, 256), 1)
    if back:
        down, across = across, down
    return jnp.where(across == 2 * (down & 127) + (down >> 7), 1.0, 0.0).astype(BF)


def expert_kernel(in_ref, columns_ref, first_ref, second_ref, out_ref, rows, hidden, done):
    order = by_expert(False)
    for b in range(3):
        both = dot(order, in_ref[b * 128 : b * 128 + 128].reshape(256, D)).astype(BF)
        rows[0, b * 128 : b * 128 + 128, :] = both[:128]
        rows[1, b * 128 : b * 128 + 128, :] = both[128:]
    for e in range(2):
        logit = dot(rows[e], columns_ref[:, e * LANES : e * LANES + LANES])
        gate = jnp.concatenate([1.0 / (1.0 + jnp.exp(-logit))] * 2, axis=1)
        for s in range(0, FF, 768):
            hidden[:, s : s + 768] = jnp.maximum(dot(rows[e], first_ref[e, :, s : s + 768]), 0.0).astype(BF)
        for s in range(0, D, 256):
            done[e, :, s : s + 256] = (gate * dot(hidden[...], second_ref[e, :, s : s + 256])).astype(BF)
    order = by_expert(True)
    for b in range(3):
        r = slice(b * 128, b * 128 + 128)
        both = jnp.concatenate([done[0, r, :], done[1, r, :]], axis=0)
        out_ref[r] = dot(order, both).astype(BF).reshape(128, 2, D)


def last_kernel(back_ref, hid0_ref, hid1_ref, wide_ref, out_hbm, out, sems):
    back = back_ref[...].reshape(SLOTS, D)
    copies = []
    for i in range(4):
        r = slice(i * 128, i * 128 + 128)
        hid_ref = (hid0_ref, hid1_ref)[i // 2]
        across = lax.broadcasted_iota(jnp.int32, (128, SLOTS), 1)
        place = jnp.concatenate([wide_ref[r, :]] * 6, axis=1)
        pick = jnp.where(across == place, 1.0, 0.0).astype(BF)
        hidden = hid_ref[i % 2 * 128 : i % 2 * 128 + 128, :].astype(F32)
        out[r, :] = (hidden + dot(pick, back)).astype(BF)
        copies.append(pltpu.make_async_copy(out.at[r, :], out_hbm.at[r, :], sems.at[i]))
        copies[-1].start()
    for copy in copies:
        copy.wait()


def params(limit):
    return pltpu.CompilerParams(vmem_limit_bytes=limit * MB)


def shape(*dims, dtype=BF):
    return jax.ShapeDtypeStruct(dims, dtype)


def cost(flops, moved, exps=0):
    return pl.CostEstimate(flops=flops, bytes_accessed=moved, transcendentals=exps)


def far(value):
    return pltpu.with_memory_space_constraint(value, pltpu.HBM)


VM = pl.BlockSpec(memory_space=pltpu.VMEM)
HB = pl.BlockSpec(memory_space=pltpu.HBM)


def call_load(x):
    return pl.pallas_call(
        load_kernel,
        out_shape=(shape(LOOK, D),) * 3,
        in_specs=[HB],
        out_specs=(VM,) * 3,
        scratch_shapes=[pltpu.SemaphoreType.DMA((2,))],
        compiler_params=params(8),
        cost_estimate=cost(10**6, MB),
        name="load",
    )(far(x))


def call_first(low, high, normed, scaling, triple, mixing, columns, row):
    return pl.pallas_call(
        first_kernel,
        out_shape=(
            shape(LOOK, D),
            shape(LOOK, 2 * D, dtype=F32),
            shape(LOOK, D),
            shape(SLOTS, D),
            shape(1, T, dtype=jnp.int32),
            shape(T, LANES, dtype=jnp.int32),
            shape(D, 2 * D),
            shape(D, D),
            shape(D, 256),
        ),
        in_specs=[VM] * 3 + [HB] * 5,
        out_specs=(VM,) * 9,
        scratch_shapes=[pltpu.VMEM((T, D), BF), pltpu.VMEM((D, D), BF)]
        + [pltpu.VMEM((T, D), BF)] * 3
        + [
            pltpu.VMEM((LOOK, D), BF),
            pltpu.VMEM((LOOK, D), BF),
            pltpu.VMEM((D, 256), BF),
            pltpu.VMEM((1, T), jnp.int32),
            pltpu.SMEM((HEADS,), F32),
            pltpu.SemaphoreType.DMA((7,)),
        ],
        compiler_params=params(16),
        cost_estimate=cost(4 * 10**9, 8 * MB),
        name="first",
    )(low, high, normed, *(far(a) for a in (scaling, triple, mixing, columns, row)))


def call_second(halo, kv, mixing, x, q0, acc0, buf1, flat):
    return pl.pallas_call(
        second_kernel,
        out_shape=(shape(SLOTS // 2, 2, D), shape(LOOK, D)),
        in_specs=[VM] * 8,
        out_specs=(VM,) * 2,
        scratch_shapes=[pltpu.VMEM((LOOK, D), BF)] * 4,
        compiler_params=params(16),
        cost_estimate=cost(30 * 10**9, 8 * MB),
        name="second",
    )(halo, kv, mixing, x, q0, acc0, buf1, flat)


def call_experts(arrived, columns, entry, exits):
    return pl.pallas_call(
        expert_kernel,
        out_shape=shape(SLOTS // 2, 2, D),
        scratch_shapes=[
            pltpu.VMEM((2, SLOTS // 2, D), BF),
            pltpu.VMEM((SLOTS // 2, FF), BF),
            pltpu.VMEM((2, SLOTS // 2, D), BF),
        ],
        compiler_params=params(14),
        cost_estimate=cost(7 * 10**9, 20 * MB),
        name="experts",
    )(arrived, columns, entry, exits)


def call_last(back, hid0, hid1, wide):
    return pl.pallas_call(
        last_kernel,
        out_shape=shape(T, D),
        in_specs=[VM] * 4,
        out_specs=HB,
        scratch_shapes=[pltpu.VMEM((T, D), BF), pltpu.SemaphoreType.DMA((4,))],
        compiler_params=params(16),
        cost_estimate=cost(6 * 10**8, 3 * MB),
        name="last",
    )(back, hid0, hid1, wide)


def exchange(rows):
    rows = rows.reshape(128, CAP, 2, D)
    return lax.all_to_all(rows, AXES, split_axis=0, concat_axis=0, tiled=True).reshape(SLOTS // 2, 2, D)


def shards(x, triple, mixing, scaling, columns, pick, entry, exits):
    low, high, normed = call_load(x)
    halo = lax.ppermute(normed, AXES, [(i, i + 1) for i in range(127)])
    first = call_first(low, high, normed, scaling, triple, mixing, columns, pick.reshape(1, T))
    q0, acc0, hid1, buf1, flat, wide, kv, mix_near, columns_near = first
    buf, hid0 = call_second(halo, kv, mix_near, low, q0, acc0, buf1, flat)
    back = exchange(call_experts(exchange(buf), columns_near, entry, exits))
    return call_last(back, hid0, hid1, wide)


def solution(mesh):
    rows = P(AXES, None)
    experts = P(AXES, None, None)
    in_specs = (rows, P(), P(), P(), P(), rows, experts, experts)
    return jax.shard_map(shards, mesh=mesh, in_specs=in_specs, out_specs=rows, check_vma=False)
```

```python
import math

import jax
import jax.numpy as jnp
from jax import lax
from jax.experimental import pallas as pl
from jax.experimental.pallas import tpu as pltpu
from jax.sharding import PartitionSpec as P

D = 768
HEADS = 12
LOOK = 256
T = 512
FF = 3072
CAP = 3
SLOTS = 768
PAIRS = HEADS // 2
LANES = 128
AXES = ("row", "col")
BF = jnp.bfloat16
F32 = jnp.float32
MB = 1 << 20


def dot(a, b):
    return jnp.dot(a, b, preferred_element_type=F32)


def dot_t(a, b):
    return lax.dot_general(a, b, (((1,), (1,)), ((), ())), preferred_element_type=F32)


def norm_rows(value):
    center = value - jnp.mean(value, axis=-1, keepdims=True)
    spread = jnp.mean(center * center, axis=-1, keepdims=True)
    return (center * lax.rsqrt(spread + 1e-05)).astype(BF)


def head_blocks():
    down = lax.shift_right_logical(lax.broadcasted_iota(jnp.int32, (256, 256), 0), 6)
    across = lax.shift_right_logical(lax.broadcasted_iota(jnp.int32, (256, 256), 1), 6)
    return jnp.where(down == across, 1.0, 0.0).astype(BF)


def head_norm(value, blocks):
    square = (value * value).astype(BF)
    return value * lax.rsqrt(dot(square, blocks) * (1.0 / 64) + 1e-06)


def triangles():
    down = lax.broadcasted_iota(jnp.int32, (128, 128), 0)
    across = lax.broadcasted_iota(jnp.int32, (128, 128), 1)
    behind = jnp.where(across >= down, 1.0, 0.0).astype(BF)
    ahead = jnp.where(across <= down, 1.0, 0.0).astype(BF)
    return behind, ahead


def half_lanes(half):
    lane = lax.broadcasted_iota(jnp.int32, (1, LANES), 1)
    mine = (lane < 64) if half == 0 else (lane >= 64)
    return jnp.where(mine, 1.0, 0.0).astype(BF)


def weigh(part):
    return jnp.exp2(part).astype(BF)


def behind_weights(scores, behind):
    top = jnp.concatenate([weigh(scores[:128, :128]) * behind, weigh(scores[:128, 128:])], axis=1)
    low = jnp.concatenate([jnp.zeros((128, 128), BF), weigh(scores[128:, 128:]) * behind], axis=1)
    return jnp.concatenate([top, low], axis=0)


def own_weights(scores, ahead):
    top = jnp.concatenate([weigh(scores[:128, :128]) * ahead, jnp.zeros((128, 128), BF)], axis=1)
    low = jnp.concatenate([weigh(scores[128:, :128]), weigh(scores[128:, 128:]) * ahead], axis=1)
    return jnp.concatenate([top, low], axis=0)


def payload(values, half, ones):
    mask = half_lanes(half)
    return jnp.concatenate([values * mask, ones * mask], axis=1)


def norm_into(source, target, count):
    def step(i, carry):
        r = pl.ds(pl.multiple_of(i * 64, 64), 64)
        target[r, :] = norm_rows(source[r, :].astype(F32))
        return carry

    lax.fori_loop(0, count // 64, step, 0)


def scale_lanes(scale_ref, group):
    lane = lax.broadcasted_iota(jnp.int32, (1, 256), 1)
    value = jnp.full((1, 256), scale_ref[4 * group], F32)
    for h in range(1, 4):
        value = jnp.where(lane >= 64 * h, scale_ref[4 * group + h], value)
    return value * (math.log2(math.e) / 64)


def places(row_ref, flat_out, wide_out):
    row = row_ref[...]
    rowf = row.astype(F32)
    rowb = jnp.broadcast_to(rowf, (LANES, T)).astype(BF)
    for r in range(0, T, 128):
        down = lax.broadcasted_iota(jnp.int32, (128, T), 0) + r
        across = lax.broadcasted_iota(jnp.int32, (128, T), 1)
        eye = jnp.where(down == across, 1.0, 0.0).astype(BF)
        wide = dot_t(eye, rowb)
        same = (jnp.concatenate([wide] * 4, axis=1) == rowf) & (across < down)
        same = jnp.where(same, 1.0, 0.0).astype(BF)
        slot = dot(same, jnp.ones((T, LANES), BF)).astype(jnp.int32)
        mine = wide.astype(jnp.int32)
        wide_out[r : r + 128, :] = (mine >> 1) * (2 * CAP) + (mine & 1) + 2 * slot
        slot_row = dot_t(jnp.ones((8, T), BF), same)[:1].astype(jnp.int32)
        part = row[:, r : r + 128]
        flat_out[:, r : r + 128] = (part >> 1) * (2 * CAP) + (part & 1) + 2 * slot_row


def device_index():
    return lax.axis_index("row") * lax.axis_size("col") + lax.axis_index("col")


def own_columns(columns):
    down = lax.broadcasted_iota(jnp.int32, (256, 256), 0)
    across = lax.broadcasted_iota(jnp.int32, (256, 256), 1)
    pick = jnp.where(down == 2 * device_index() + (across >> 7), 1.0, 0.0).astype(BF)
    return dot(columns, pick).astype(BF)


def finish(ctx, mix_ref, x_ref, hid_out, rou_out):
    for r in range(0, LOOK, 128):
        mixed = dot(ctx[r : r + 128, :], mix_ref[...])
        for s in range(r, r + 128, 32):
            hidden = (x_ref[s : s + 32, :].astype(F32) + mixed[s - r : s - r + 32, :]).astype(BF)
            hid_out[s : s + 32, :] = hidden
            rou_out[s : s + 32, :] = norm_rows(hidden.astype(F32))


def dispatch(flat, at, routed):
    place = lax.broadcasted_iota(jnp.int32, (256, LOOK), 0) + at
    return dot(jnp.where(place == flat, 1.0, 0.0).astype(BF), routed[...]).astype(BF)


def apart(work):
    def step(i, carry):
        work()
        return carry

    lax.fori_loop(0, jnp.minimum(device_index(), 0) + 1, step, 0)


def load_kernel(x_hbm, low_out, high_out, normed_out, sems):
    high = pltpu.make_async_copy(x_hbm.at[pl.ds(LOOK, LOOK), :], high_out, sems.at[0])
    low = pltpu.make_async_copy(x_hbm.at[pl.ds(0, LOOK), :], low_out, sems.at[1])
    high.start()
    low.start()
    high.wait()
    for r in range(0, LOOK, 32):
        normed_out[r : r + 32, :] = norm_rows(high_out[r : r + 32, :].astype(F32))
    apart(low.wait)


def first_kernel(
    low_ref, high_ref, normed_ref, scale_hbm, w_hbm, mix_hbm, columns_hbm, row_hbm,
    q_out, acc_out, hid_out, buf_out, flat_out, wide_out, kv_out, mix_ref, columns_out,
    normed, wq, q_s, k_s, v_s, ctx, routed, columns_ref, row_ref, scale_ref, sems,
):
    early = [
        pltpu.make_async_copy(row_hbm, row_ref, sems.at[5]),
        pltpu.make_async_copy(columns_hbm, columns_ref, sems.at[3]),
    ]
    dense = [
        pltpu.make_async_copy(w_hbm.at[:, pl.ds(0, D)], wq, sems.at[1]),
        pltpu.make_async_copy(w_hbm.at[:, pl.ds(D, 2 * D)], kv_out, sems.at[2]),
        pltpu.make_async_copy(scale_hbm, scale_ref, sems.at[6]),
    ]
    mix = [pltpu.make_async_copy(mix_hbm, mix_ref, sems.at[4])]
    for copy in early + dense + mix:
        copy.start()
    for copy in early:
        copy.wait()

    def prepare():
        for r in range(0, LOOK, 32):
            normed[r : r + 32, :] = norm_rows(low_ref[r : r + 32, :].astype(F32))
        normed[LOOK:, :] = normed_ref[...]
        places(row_ref, flat_out, wide_out)
        columns_out[...] = own_columns(columns_ref[...])

    apart(prepare)
    for copy in dense:
        copy.wait()
    blocks = head_blocks()
    for g in range(3):
        c = slice(g * 256, g * 256 + 256)
        value = head_norm(dot(normed[...], wq[:, c]), blocks)
        q_s[:, c] = (value * scale_lanes(scale_ref, g)).astype(BF)
        k_s[:, c] = head_norm(dot(normed[...], kv_out[:, c]), blocks).astype(BF)
        v_s[:, c] = dot(normed[...], kv_out[:, D + g * 256 : D + g * 256 + 256]).astype(BF)
    q_out[...] = q_s[:LOOK, :]
    behind, ahead = triangles()
    ones = jnp.ones((LOOK, LANES), BF)
    for pair in range(PAIRS):
        c = slice(pair * LANES, pair * LANES + LANES)
        low = jnp.zeros((LOOK, 256), F32)
        high = jnp.zeros((LOOK, 256), F32)
        for half in range(2):
            mask = half_lanes(half)
            q0 = q_s[:LOOK, c] * mask
            q1 = q_s[LOOK:, c] * mask
            k0 = k_s[:LOOK, c]
            k1 = k_s[LOOK:, c]
            v0 = payload(v_s[:LOOK, c], half, ones)
            v1 = payload(v_s[LOOK:, c], half, ones)
            low += dot(own_weights(dot_t(q0, k0), ahead), v0)
            both = jnp.concatenate([behind_weights(dot_t(q1, k0), behind), own_weights(dot_t(q1, k1), ahead)], axis=1)
            high += dot(both, jnp.concatenate([v0, v1], axis=0))
        acc_out[:, pair * 256 : pair * 256 + 256] = low
        ctx[:, c] = (high[:, :LANES] / high[:, LANES:]).astype(BF)
    apart(mix[0].wait)
    finish(ctx, mix_ref, high_ref, hid_out, routed)
    for s in range(0, SLOTS, 256):
        buf_out[s : s + 256, :] = dispatch(flat_out[:, LOOK:], s, routed)


def second_kernel(
    halo_ref, kv_ref, mix_ref, x_ref, q_ref, acc_ref, buf_ref, flat_ref,
    buf_out, hid_out, k_s, v_s, ctx, routed,
):
    blocks = head_blocks()
    for g in range(3):
        c = slice(g * 256, g * 256 + 256)
        k_s[:, c] = head_norm(dot(halo_ref[...], kv_ref[:, c]), blocks).astype(BF)
        v_s[:, c] = dot(halo_ref[...], kv_ref[:, D + g * 256 : D + g * 256 + 256]).astype(BF)
    behind, _ = triangles()
    ones = jnp.full((LOOK, LANES), jnp.minimum(device_index(), 1).astype(F32)).astype(BF)
    for pair in range(PAIRS):
        c = slice(pair * LANES, pair * LANES + LANES)
        low = acc_ref[:, pair * 256 : pair * 256 + 256]
        part = []
        for half in range(2):
            q0 = q_ref[:, c] * half_lanes(half)
            part.append(behind_weights(dot_t(q0, k_s[:, c]), behind))
        both = jnp.concatenate([payload(v_s[:, c], 0, ones), payload(v_s[:, c], 1, ones)], axis=0)
        low += dot(jnp.concatenate(part, axis=1), both)
        ctx[:, c] = (low[:, :LANES] / low[:, LANES:]).astype(BF)
    finish(ctx, mix_ref, x_ref, hid_out, routed)
    for s in range(0, SLOTS, 256):
        rows = dispatch(flat_ref[:, :LOOK], s, routed) + buf_ref[s : s + 256, :]
        buf_out[s // 2 : s // 2 + 128] = rows.reshape(128, 2, D)


def by_expert(back):
    down = lax.broadcasted_iota(jnp.int32, (256, 256), 0)
    across = lax.broadcasted_iota(jnp.int32, (256, 256), 1)
    if back:
        down, across = across, down
    return jnp.where(across == 2 * (down & 127) + (down >> 7), 1.0, 0.0).astype(BF)


def expert_kernel(in_ref, columns_ref, first_ref, second_ref, out_ref, rows, hidden, done):
    order = by_expert(False)
    for b in range(3):
        both = dot(order, in_ref[b * 128 : b * 128 + 128].reshape(256, D)).astype(BF)
        rows[0, b * 128 : b * 128 + 128, :] = both[:128]
        rows[1, b * 128 : b * 128 + 128, :] = both[128:]
    for e in range(2):
        logit = dot(rows[e], columns_ref[:, e * LANES : e * LANES + LANES])
        gate = jnp.concatenate([1.0 / (1.0 + jnp.exp(-logit))] * 2, axis=1)
        for s in range(0, FF, 768):
            hidden[:, s : s + 768] = jnp.maximum(dot(rows[e], first_ref[e, :, s : s + 768]), 0.0).astype(BF)
        for s in range(0, D, 256):
            done[e, :, s : s + 256] = (gate * dot(hidden[...], second_ref[e, :, s : s + 256])).astype(BF)
    order = by_expert(True)
    for b in range(3):
        r = slice(b * 128, b * 128 + 128)
        both = jnp.concatenate([done[0, r, :], done[1, r, :]], axis=0)
        out_ref[r] = dot(order, both).astype(BF).reshape(128, 2, D)


def last_kernel(back_ref, hid0_ref, hid1_ref, wide_ref, out_hbm, out, sems):
    back = back_ref[...].reshape(SLOTS, D)
    copies = []
    for i in range(4):
        r = slice(i * 128, i * 128 + 128)
        hid_ref = (hid0_ref, hid1_ref)[i // 2]
        across = lax.broadcasted_iota(jnp.int32, (128, SLOTS), 1)
        place = jnp.concatenate([wide_ref[r, :]] * 6, axis=1)
        pick = jnp.where(across == place, 1.0, 0.0).astype(BF)
        hidden = hid_ref[i % 2 * 128 : i % 2 * 128 + 128, :].astype(F32)
        out[r, :] = (hidden + dot(pick, back)).astype(BF)
        copies.append(pltpu.make_async_copy(out.at[r, :], out_hbm.at[r, :], sems.at[i]))
        copies[-1].start()
    for copy in copies:
        copy.wait()


def params(limit):
    return pltpu.CompilerParams(vmem_limit_bytes=limit * MB)


def shape(*dims, dtype=BF):
    return jax.ShapeDtypeStruct(dims, dtype)


def cost(flops, moved, exps=0):
    return pl.CostEstimate(flops=flops, bytes_accessed=moved, transcendentals=exps)


def far(value):
    return pltpu.with_memory_space_constraint(value, pltpu.HBM)


VM = pl.BlockSpec(memory_space=pltpu.VMEM)
HB = pl.BlockSpec(memory_space=pltpu.HBM)


def call_load(x):
    return pl.pallas_call(
        load_kernel,
        out_shape=(shape(LOOK, D),) * 3,
        in_specs=[HB],
        out_specs=(VM,) * 3,
        scratch_shapes=[pltpu.SemaphoreType.DMA((2,))],
        compiler_params=params(8),
        cost_estimate=cost(10**6, MB),
        name="load",
    )(far(x))


def call_first(low, high, normed, scaling, triple, mixing, columns, row):
    return pl.pallas_call(
        first_kernel,
        out_shape=(
            shape(LOOK, D),
            shape(LOOK, 2 * D, dtype=F32),
            shape(LOOK, D),
            shape(SLOTS, D),
            shape(1, T, dtype=jnp.int32),
            shape(T, LANES, dtype=jnp.int32),
            shape(D, 2 * D),
            shape(D, D),
            shape(D, 256),
        ),
        in_specs=[VM] * 3 + [HB] * 5,
        out_specs=(VM,) * 9,
        scratch_shapes=[pltpu.VMEM((T, D), BF), pltpu.VMEM((D, D), BF)]
        + [pltpu.VMEM((T, D), BF)] * 3
        + [
            pltpu.VMEM((LOOK, D), BF),
            pltpu.VMEM((LOOK, D), BF),
            pltpu.VMEM((D, 256), BF),
            pltpu.VMEM((1, T), jnp.int32),
            pltpu.SMEM((HEADS,), F32),
            pltpu.SemaphoreType.DMA((7,)),
        ],
        compiler_params=params(16),
        cost_estimate=cost(4 * 10**9, 8 * MB),
        name="first",
    )(low, high, normed, *(far(a) for a in (scaling, triple, mixing, columns, row)))


def call_second(halo, kv, mixing, x, q0, acc0, buf1, flat):
    return pl.pallas_call(
        second_kernel,
        out_shape=(shape(SLOTS // 2, 2, D), shape(LOOK, D)),
        in_specs=[VM] * 8,
        out_specs=(VM,) * 2,
        scratch_shapes=[pltpu.VMEM((LOOK, D), BF)] * 4,
        compiler_params=params(16),
        cost_estimate=cost(30 * 10**9, 8 * MB),
        name="second",
    )(halo, kv, mixing, x, q0, acc0, buf1, flat)


def call_experts(arrived, columns, entry, exits):
    return pl.pallas_call(
        expert_kernel,
        out_shape=shape(SLOTS // 2, 2, D),
        scratch_shapes=[
            pltpu.VMEM((2, SLOTS // 2, D), BF),
            pltpu.VMEM((SLOTS // 2, FF), BF),
            pltpu.VMEM((2, SLOTS // 2, D), BF),
        ],
        compiler_params=params(14),
        cost_estimate=cost(7 * 10**9, 20 * MB),
        name="experts",
    )(arrived, columns, entry, exits)


def call_last(back, hid0, hid1, wide):
    return pl.pallas_call(
        last_kernel,
        out_shape=shape(T, D),
        in_specs=[VM] * 4,
        out_specs=HB,
        scratch_shapes=[pltpu.VMEM((T, D), BF), pltpu.SemaphoreType.DMA((4,))],
        compiler_params=params(16),
        cost_estimate=cost(6 * 10**8, 3 * MB),
        name="last",
    )(back, hid0, hid1, wide)


def exchange(rows):
    rows = rows.reshape(128, CAP, 2, D)
    return lax.all_to_all(rows, AXES, split_axis=0, concat_axis=0, tiled=True).reshape(SLOTS // 2, 2, D)


def shards(x, triple, mixing, scaling, columns, pick, entry, exits):
    low, high, normed = call_load(x)
    halo = lax.ppermute(normed, AXES, [(i, i + 1) for i in range(127)])
    first = call_first(low, high, normed, scaling, triple, mixing, columns, pick.reshape(1, T))
    q0, acc0, hid1, buf1, flat, wide, kv, mix_near, columns_near = first
    buf, hid0 = call_second(halo, kv, mix_near, low, q0, acc0, buf1, flat)
    back = exchange(call_experts(exchange(buf), columns_near, entry, exits))
    return call_last(back, hid0, hid1, wide)


def solution(mesh):
    rows = P(AXES, None)
    experts = P(AXES, None, None)
    in_specs = (rows, P(), P(), P(), P(), rows, experts, experts)
    return jax.shard_map(shards, mesh=mesh, in_specs=in_specs, out_specs=rows, check_vma=False)
```

```python
import math

import jax
import jax.numpy as jnp
from jax import lax
from jax.experimental import pallas as pl
from jax.experimental.pallas import tpu as pltpu
from jax.sharding import PartitionSpec as P

D = 768
HEADS = 12
LOOK = 256
T = 512
FF = 3072
CAP = 3
SLOTS = 768
PAIRS = HEADS // 2
LANES = 128
AXES = ("row", "col")
BF = jnp.bfloat16
F32 = jnp.float32
MB = 1 << 20


def dot(a, b):
    return jnp.dot(a, b, preferred_element_type=F32)


def dot_t(a, b):
    return lax.dot_general(a, b, (((1,), (1,)), ((), ())), preferred_element_type=F32)


def norm_rows(value):
    center = value - jnp.mean(value, axis=-1, keepdims=True)
    spread = jnp.mean(center * center, axis=-1, keepdims=True)
    return (center * lax.rsqrt(spread + 1e-05)).astype(BF)


def head_blocks():
    down = lax.shift_right_logical(lax.broadcasted_iota(jnp.int32, (256, 256), 0), 6)
    across = lax.shift_right_logical(lax.broadcasted_iota(jnp.int32, (256, 256), 1), 6)
    return jnp.where(down == across, 1.0, 0.0).astype(BF)


def head_norm(value, blocks):
    square = (value * value).astype(BF)
    return value * lax.rsqrt(dot(square, blocks) * (1.0 / 64) + 1e-06)


def triangles():
    down = lax.broadcasted_iota(jnp.int32, (128, 128), 0)
    across = lax.broadcasted_iota(jnp.int32, (128, 128), 1)
    behind = jnp.where(across >= down, 1.0, 0.0).astype(BF)
    ahead = jnp.where(across <= down, 1.0, 0.0).astype(BF)
    return behind, ahead


def half_lanes(half):
    lane = lax.broadcasted_iota(jnp.int32, (1, LANES), 1)
    mine = (lane < 64) if half == 0 else (lane >= 64)
    return jnp.where(mine, 1.0, 0.0).astype(BF)


def weigh(part):
    return jnp.exp2(part).astype(BF)


def behind_weights(scores, behind):
    top = jnp.concatenate([weigh(scores[:128, :128]) * behind, weigh(scores[:128, 128:])], axis=1)
    low = jnp.concatenate([jnp.zeros((128, 128), BF), weigh(scores[128:, 128:]) * behind], axis=1)
    return jnp.concatenate([top, low], axis=0)


def own_weights(scores, ahead):
    top = jnp.concatenate([weigh(scores[:128, :128]) * ahead, jnp.zeros((128, 128), BF)], axis=1)
    low = jnp.concatenate([weigh(scores[128:, :128]), weigh(scores[128:, 128:]) * ahead], axis=1)
    return jnp.concatenate([top, low], axis=0)


def payload(values, half, ones):
    mask = half_lanes(half)
    return jnp.concatenate([values * mask, ones * mask], axis=1)


def norm_into(source, target, count):
    def step(i, carry):
        r = pl.ds(pl.multiple_of(i * 64, 64), 64)
        target[r, :] = norm_rows(source[r, :].astype(F32))
        return carry

    lax.fori_loop(0, count // 64, step, 0)


def scale_lanes(scale_ref, group):
    lane = lax.broadcasted_iota(jnp.int32, (1, 256), 1)
    value = jnp.full((1, 256), scale_ref[4 * group], F32)
    for h in range(1, 4):
        value = jnp.where(lane >= 64 * h, scale_ref[4 * group + h], value)
    return value * (math.log2(math.e) / 64)


def places(row_ref, flat_out, wide_out):
    row = row_ref[...]
    rowf = row.astype(F32)
    rowb = jnp.broadcast_to(rowf, (LANES, T)).astype(BF)
    for r in range(0, T, 128):
        down = lax.broadcasted_iota(jnp.int32, (128, T), 0) + r
        across = lax.broadcasted_iota(jnp.int32, (128, T), 1)
        eye = jnp.where(down == across, 1.0, 0.0).astype(BF)
        wide = dot_t(eye, rowb)
        same = (jnp.concatenate([wide] * 4, axis=1) == rowf) & (across < down)
        same = jnp.where(same, 1.0, 0.0).astype(BF)
        slot = dot(same, jnp.ones((T, LANES), BF)).astype(jnp.int32)
        mine = wide.astype(jnp.int32)
        wide_out[r : r + 128, :] = (mine >> 1) * (2 * CAP) + (mine & 1) + 2 * slot
        slot_row = dot_t(jnp.ones((8, T), BF), same)[:1].astype(jnp.int32)
        part = row[:, r : r + 128]
        flat_out[:, r : r + 128] = (part >> 1) * (2 * CAP) + (part & 1) + 2 * slot_row


def device_index():
    return lax.axis_index("row") * lax.axis_size("col") + lax.axis_index("col")


def own_columns(columns):
    down = lax.broadcasted_iota(jnp.int32, (256, 256), 0)
    across = lax.broadcasted_iota(jnp.int32, (256, 256), 1)
    pick = jnp.where(down == 2 * device_index() + (across >> 7), 1.0, 0.0).astype(BF)
    return dot(columns, pick).astype(BF)


def finish(ctx, mix_ref, x_ref, hid_out, rou_out):
    for r in range(0, LOOK, 128):
        mixed = dot(ctx[r : r + 128, :], mix_ref[...])
        for s in range(r, r + 128, 32):
            hidden = (x_ref[s : s + 32, :].astype(F32) + mixed[s - r : s - r + 32, :]).astype(BF)
            hid_out[s : s + 32, :] = hidden
            rou_out[s : s + 32, :] = norm_rows(hidden.astype(F32))


def dispatch(flat, at, routed):
    place = lax.broadcasted_iota(jnp.int32, (256, LOOK), 0) + at
    return dot(jnp.where(place == flat, 1.0, 0.0).astype(BF), routed[...]).astype(BF)


def apart(work):
    def step(i, carry):
        work()
        return carry

    lax.fori_loop(0, jnp.minimum(device_index(), 0) + 1, step, 0)


def load_kernel(x_hbm, high_out, normed_out, sem):
    high = pltpu.make_async_copy(x_hbm.at[pl.ds(LOOK, LOOK), :], high_out, sem)
    high.start()
    high.wait()
    for r in range(0, LOOK, 32):
        normed_out[r : r + 32, :] = norm_rows(high_out[r : r + 32, :].astype(F32))


def first_kernel(
    high_ref, normed_ref, x_hbm, scale_hbm, w_hbm, mix_hbm, columns_hbm, row_hbm,
    q_out, acc_out, hid_out, buf_out, flat_out, wide_out, low_ref, kv_out, mix_ref, columns_out,
    normed, wq, q_s, k_s, v_s, ctx, routed, columns_ref, row_ref, scale_ref, sems,
):
    early = [
        pltpu.make_async_copy(x_hbm.at[pl.ds(0, LOOK), :], low_ref, sems.at[0]),
        pltpu.make_async_copy(row_hbm, row_ref, sems.at[5]),
        pltpu.make_async_copy(columns_hbm, columns_ref, sems.at[3]),
    ]
    dense = [
        pltpu.make_async_copy(w_hbm.at[:, pl.ds(0, D)], wq, sems.at[1]),
        pltpu.make_async_copy(w_hbm.at[:, pl.ds(D, 2 * D)], kv_out, sems.at[2]),
        pltpu.make_async_copy(scale_hbm, scale_ref, sems.at[6]),
    ]
    mix = [pltpu.make_async_copy(mix_hbm, mix_ref, sems.at[4])]
    for copy in early + dense + mix:
        copy.start()
    for copy in early:
        copy.wait()

    def prepare():
        for r in range(0, LOOK, 32):
            normed[r : r + 32, :] = norm_rows(low_ref[r : r + 32, :].astype(F32))
        normed[LOOK:, :] = normed_ref[...]
        places(row_ref, flat_out, wide_out)
        columns_out[...] = own_columns(columns_ref[...])

    apart(prepare)
    for copy in dense:
        copy.wait()
    blocks = head_blocks()
    for g in range(3):
        c = slice(g * 256, g * 256 + 256)
        value = head_norm(dot(normed[...], wq[:, c]), blocks)
        q_s[:, c] = (value * scale_lanes(scale_ref, g)).astype(BF)
        k_s[:, c] = head_norm(dot(normed[...], kv_out[:, c]), blocks).astype(BF)
        v_s[:, c] = dot(normed[...], kv_out[:, D + g * 256 : D + g * 256 + 256]).astype(BF)
    q_out[...] = q_s[:LOOK, :]
    behind, ahead = triangles()
    ones = jnp.ones((LOOK, LANES), BF)
    for pair in range(PAIRS):
        c = slice(pair * LANES, pair * LANES + LANES)
        low = jnp.zeros((LOOK, 256), F32)
        high = jnp.zeros((LOOK, 256), F32)
        for half in range(2):
            mask = half_lanes(half)
            q0 = q_s[:LOOK, c] * mask
            q1 = q_s[LOOK:, c] * mask
            k0 = k_s[:LOOK, c]
            k1 = k_s[LOOK:, c]
            v0 = payload(v_s[:LOOK, c], half, ones)
            v1 = payload(v_s[LOOK:, c], half, ones)
            low += dot(own_weights(dot_t(q0, k0), ahead), v0)
            both = jnp.concatenate([behind_weights(dot_t(q1, k0), behind), own_weights(dot_t(q1, k1), ahead)], axis=1)
            high += dot(both, jnp.concatenate([v0, v1], axis=0))
        acc_out[:, pair * 256 : pair * 256 + 256] = low
        ctx[:, c] = (high[:, :LANES] / high[:, LANES:]).astype(BF)
    apart(mix[0].wait)
    finish(ctx, mix_ref, high_ref, hid_out, routed)
    for s in range(0, SLOTS, 256):
        buf_out[s : s + 256, :] = dispatch(flat_out[:, LOOK:], s, routed)


def second_kernel(
    halo_ref, kv_ref, mix_ref, x_ref, q_ref, acc_ref, buf_ref, flat_ref,
    buf_out, hid_out, k_s, v_s, ctx, routed,
):
    blocks = head_blocks()
    for g in range(3):
        c = slice(g * 256, g * 256 + 256)
        k_s[:, c] = head_norm(dot(halo_ref[...], kv_ref[:, c]), blocks).astype(BF)
        v_s[:, c] = dot(halo_ref[...], kv_ref[:, D + g * 256 : D + g * 256 + 256]).astype(BF)
    behind, _ = triangles()
    ones = jnp.full((LOOK, LANES), jnp.minimum(device_index(), 1).astype(F32)).astype(BF)
    for pair in range(PAIRS):
        c = slice(pair * LANES, pair * LANES + LANES)
        low = acc_ref[:, pair * 256 : pair * 256 + 256]
        part = []
        for half in range(2):
            q0 = q_ref[:, c] * half_lanes(half)
            part.append(behind_weights(dot_t(q0, k_s[:, c]), behind))
        both = jnp.concatenate([payload(v_s[:, c], 0, ones), payload(v_s[:, c], 1, ones)], axis=0)
        low += dot(jnp.concatenate(part, axis=1), both)
        ctx[:, c] = (low[:, :LANES] / low[:, LANES:]).astype(BF)
    finish(ctx, mix_ref, x_ref, hid_out, routed)
    for s in range(0, SLOTS, 256):
        rows = dispatch(flat_ref[:, :LOOK], s, routed) + buf_ref[s : s + 256, :]
        buf_out[s // 2 : s // 2 + 128] = rows.reshape(128, 2, D)


def by_expert(back):
    down = lax.broadcasted_iota(jnp.int32, (256, 256), 0)
    across = lax.broadcasted_iota(jnp.int32, (256, 256), 1)
    if back:
        down, across = across, down
    return jnp.where(across == 2 * (down & 127) + (down >> 7), 1.0, 0.0).astype(BF)


def expert_kernel(in_ref, columns_ref, first_ref, second_ref, out_ref, rows, hidden, done):
    order = by_expert(False)
    for b in range(3):
        both = dot(order, in_ref[b * 128 : b * 128 + 128].reshape(256, D)).astype(BF)
        rows[0, b * 128 : b * 128 + 128, :] = both[:128]
        rows[1, b * 128 : b * 128 + 128, :] = both[128:]
    for e in range(2):
        logit = dot(rows[e], columns_ref[:, e * LANES : e * LANES + LANES])
        gate = jnp.concatenate([1.0 / (1.0 + jnp.exp(-logit))] * 2, axis=1)
        for s in range(0, FF, 768):
            hidden[:, s : s + 768] = jnp.maximum(dot(rows[e], first_ref[e, :, s : s + 768]), 0.0).astype(BF)
        for s in range(0, D, 256):
            done[e, :, s : s + 256] = (gate * dot(hidden[...], second_ref[e, :, s : s + 256])).astype(BF)
    order = by_expert(True)
    for b in range(3):
        r = slice(b * 128, b * 128 + 128)
        both = jnp.concatenate([done[0, r, :], done[1, r, :]], axis=0)
        out_ref[r] = dot(order, both).astype(BF).reshape(128, 2, D)


def last_kernel(back_ref, hid0_ref, hid1_ref, wide_ref, out_hbm, out, sems):
    back = back_ref[...].reshape(SLOTS, D)
    copies = []
    for i in range(4):
        r = slice(i * 128, i * 128 + 128)
        hid_ref = (hid0_ref, hid1_ref)[i // 2]
        across = lax.broadcasted_iota(jnp.int32, (128, SLOTS), 1)
        place = jnp.concatenate([wide_ref[r, :]] * 6, axis=1)
        pick = jnp.where(across == place, 1.0, 0.0).astype(BF)
        hidden = hid_ref[i % 2 * 128 : i % 2 * 128 + 128, :].astype(F32)
        out[r, :] = (hidden + dot(pick, back)).astype(BF)
        copies.append(pltpu.make_async_copy(out.at[r, :], out_hbm.at[r, :], sems.at[i]))
        copies[-1].start()
    for copy in copies:
        copy.wait()


def params(limit):
    return pltpu.CompilerParams(vmem_limit_bytes=limit * MB)


def shape(*dims, dtype=BF):
    return jax.ShapeDtypeStruct(dims, dtype)


def cost(flops, moved, exps=0):
    return pl.CostEstimate(flops=flops, bytes_accessed=moved, transcendentals=exps)


def far(value):
    return pltpu.with_memory_space_constraint(value, pltpu.HBM)


VM = pl.BlockSpec(memory_space=pltpu.VMEM)
HB = pl.BlockSpec(memory_space=pltpu.HBM)


def call_load(x):
    return pl.pallas_call(
        load_kernel,
        out_shape=(shape(LOOK, D),) * 2,
        in_specs=[HB],
        out_specs=(VM,) * 2,
        scratch_shapes=[pltpu.SemaphoreType.DMA],
        compiler_params=params(8),
        cost_estimate=cost(10**6, MB),
        name="load",
    )(far(x))


def call_first(high, normed, x, scaling, triple, mixing, columns, row):
    return pl.pallas_call(
        first_kernel,
        out_shape=(
            shape(LOOK, D),
            shape(LOOK, 2 * D, dtype=F32),
            shape(LOOK, D),
            shape(SLOTS, D),
            shape(1, T, dtype=jnp.int32),
            shape(T, LANES, dtype=jnp.int32),
            shape(LOOK, D),
            shape(D, 2 * D),
            shape(D, D),
            shape(D, 256),
        ),
        in_specs=[VM] * 2 + [HB] * 6,
        out_specs=(VM,) * 10,
        scratch_shapes=[pltpu.VMEM((T, D), BF), pltpu.VMEM((D, D), BF)]
        + [pltpu.VMEM((T, D), BF)] * 3
        + [
            pltpu.VMEM((LOOK, D), BF),
            pltpu.VMEM((LOOK, D), BF),
            pltpu.VMEM((D, 256), BF),
            pltpu.VMEM((1, T), jnp.int32),
            pltpu.SMEM((HEADS,), F32),
            pltpu.SemaphoreType.DMA((7,)),
        ],
        compiler_params=params(16),
        cost_estimate=cost(4 * 10**9, 8 * MB),
        name="first",
    )(high, normed, *(far(a) for a in (x, scaling, triple, mixing, columns, row)))


def call_second(halo, kv, mixing, x, q0, acc0, buf1, flat):
    return pl.pallas_call(
        second_kernel,
        out_shape=(shape(SLOTS // 2, 2, D), shape(LOOK, D)),
        in_specs=[VM] * 8,
        out_specs=(VM,) * 2,
        scratch_shapes=[pltpu.VMEM((LOOK, D), BF)] * 4,
        compiler_params=params(16),
        cost_estimate=cost(30 * 10**9, 8 * MB),
        name="second",
    )(halo, kv, mixing, x, q0, acc0, buf1, flat)


def call_experts(arrived, columns, entry, exits):
    return pl.pallas_call(
        expert_kernel,
        out_shape=shape(SLOTS // 2, 2, D),
        scratch_shapes=[
            pltpu.VMEM((2, SLOTS // 2, D), BF),
            pltpu.VMEM((SLOTS // 2, FF), BF),
            pltpu.VMEM((2, SLOTS // 2, D), BF),
        ],
        compiler_params=params(14),
        cost_estimate=cost(7 * 10**9, 20 * MB),
        name="experts",
    )(arrived, columns, entry, exits)


def call_last(back, hid0, hid1, wide):
    return pl.pallas_call(
        last_kernel,
        out_shape=shape(T, D),
        in_specs=[VM] * 4,
        out_specs=HB,
        scratch_shapes=[pltpu.VMEM((T, D), BF), pltpu.SemaphoreType.DMA((4,))],
        compiler_params=params(16),
        cost_estimate=cost(6 * 10**8, 3 * MB),
        name="last",
    )(back, hid0, hid1, wide)


def exchange(rows):
    rows = rows.reshape(128, CAP, 2, D)
    return lax.all_to_all(rows, AXES, split_axis=0, concat_axis=0, tiled=True).reshape(SLOTS // 2, 2, D)


def shards(x, triple, mixing, scaling, columns, pick, entry, exits):
    high, normed = call_load(x)
    halo = lax.ppermute(normed, AXES, [(i, i + 1) for i in range(127)])
    first = call_first(high, normed, x, scaling, triple, mixing, columns, pick.reshape(1, T))
    q0, acc0, hid1, buf1, flat, wide, low, kv, mix_near, columns_near = first
    buf, hid0 = call_second(halo, kv, mix_near, low, q0, acc0, buf1, flat)
    back = exchange(call_experts(exchange(buf), columns_near, entry, exits))
    return call_last(back, hid0, hid1, wide)


def solution(mesh):
    rows = P(AXES, None)
    experts = P(AXES, None, None)
    in_specs = (rows, P(), P(), P(), P(), rows, experts, experts)
    return jax.shard_map(shards, mesh=mesh, in_specs=in_specs, out_specs=rows, check_vma=False)
```
